32 devices in a mesh: grain: 8 (over z, y), cell: 4 (over x, core).
Axes of the slice: x: 2, y: 2, z: 4, core: 2. Of those that a mesh axis runs over, the one named last changes fastest.
Arguments:
- displacement: float32 [1024, 3, 768], P(('grain', 'cell')), may hold values from -0.1 to 0.1
- velocity: float32 [1024, 3, 768], P(('grain', 'cell')), may hold values from -6 to 6
- centers: float32 [3, 1024], P(None, ('grain', 'cell')), may hold values from -4 to 4
- tile_list: int32 [1024, 4, 2], P(('grain', 'cell')), may hold values from 0 to 5
- broken_bits: int32 [1024, 4, 2048], P(('grain', 'cell')), may hold values from 0 to 255, as said below
- surface_nodes: int32 [1024, 512], P(('grain', 'cell')), may hold values from 0 to 767, as said below
- send_order: int32 [32, 128], P(('grain', 'cell')), may hold values from 0 to 127, each once within a row
- pair_list: int32 [32, 128, 2], P(('grain', 'cell')), may hold values from 0 to 127
- pair_count: int32 [32], P(('grain', 'cell')), may hold values from 1 to 128, 2048 in all
Outputs:
- force: float32 [1024, 3, 768], P(('grain', 'cell'))
- new_velocity: float32 [1024, 3, 768], P(('grain', 'cell'))
The draws below stay inside these ranges and needn't reach their ends.
Inputs may be any that keep to these rules, and one draw needn't show every extreme that they name: `surface_nodes`: within a grain the 512 surface node indices are distinct. `send_order`: each row is a permutation of the device's 128 surface blocks; position p goes to device p div 4, so every device receives exactly 4 blocks from each device. `broken_bits`: each word packs 8 broken flags, any bit pattern.
All inputs are finite; a program needn't handle non-finite values. No bound on the sum of `pair_count` on one device may be relied on, other than what follows from the above.
Results may differ from the reference program's by a relative error of at most 0.0003.
Values sent between devices are 32-bit elements; how exact they have to be, the bound alone decides.
A program may use at most 64 MiB of HBM per device.

```python
import math
import jax
import jax.numpy as jnp
import numpy as np
from jax import lax

NODES = 768
BLK = 128
SB = 4
TILES_G = 4
PAIRS_DEV = 128
OWNERS = 32
GRAINS = 1024
SBLK_DEV = 128
SURF = 512
CAP = 4
WORDS = 2048


def draw_broken_bits(key, part):
    shape_all = (GRAINS, TILES_G, WORDS)
    keys = jax.random.split(jax.random.fold_in(key, 7), 3)
    first_word = jax.random.randint(keys[0], shape_all, 0, 256, dtype=jnp.int32)
    second_word = jax.random.randint(keys[1], shape_all, 0, 256, dtype=jnp.int32)
    third_word = jax.random.randint(keys[2], shape_all, 0, 256, dtype=jnp.int32)
    combined = first_word & second_word & third_word
    return combined.at[0, 0, 0].set(255)


def draw_surface_nodes(key, part):
    keys = jax.random.split(jax.random.fold_in(key, 13), GRAINS)

    def one_grain(grain_key):
        return jax.random.permutation(grain_key, NODES)[:SURF].astype(jnp.int32)
    return jax.vmap(one_grain)(keys)


def touch_ends(values, stream_key, smallest, top_value):
    dims = values.shape
    spot = [jax.random.randint(jax.random.fold_in(stream_key, axis), (), 0, dims[axis]) for axis in range(len(dims))]
    values = values.at[tuple(spot)].set(smallest)
    longest = dims.index(max(dims))
    spot[longest] = (spot[longest] + 1) % dims[longest]
    return values.at[tuple(spot)].set(top_value)


def shard_levels(stream_key, shape, cuts, low, top_value):
    def one(position, blocks):
        draws = jax.random.uniform(jax.random.fold_in(jax.random.fold_in(stream_key, 6), position), (blocks,), jnp.float32, low / len(cuts), top_value / len(cuts))
        return jnp.repeat(jnp.exp(draws), shape[position] // blocks).reshape((-1,) + (1,) * (len(shape) - position - 1))

    loudness = one(*cuts[0])
    for cut in cuts[1:]:
        loudness = loudness * one(*cut)
    return loudness


def length_profile(amount, total, most, slope):
    portions = [(1 << 20) // math.isqrt(grade ** slope) + 1 for grade in range(2, amount + 1)]
    spare, holding = total - most - (amount - 1), [1] * (amount - 1)
    while spare > 0:
        movable = [i for i in range(amount - 1) if holding[i] < most]
        mass, left = sum([portions[i] for i in movable]), spare
        for i in movable:
            extra = min(most - holding[i], max(1, left * portions[i] // mass), spare)
            holding[i] = holding[i] + extra
            spare = spare - extra
    return np.array([most] + holding)


def ragged_sizes(stream_key, count, total, bound, skew):
    if count == 2:
        one = jax.random.randint(stream_key, (), max(1, total - bound), min(bound, total - 1) + 1)
        return jnp.stack([one, total - one])
    lengths = jnp.asarray(length_profile(count, total, bound, skew), jnp.int32)
    pairs = (count - 1) // 2
    source_of, taker = lengths[1:1 + 2 * pairs:2], lengths[2:2 + 2 * pairs:2]
    margin = jnp.minimum(source_of - 1, bound - taker)
    shifted = jax.random.randint(jax.random.fold_in(stream_key, 1), (pairs,), 0, 1 << 20) % (margin + 1)
    lengths = lengths.at[1:1 + 2 * pairs:2].set(source_of - shifted).at[2:2 + 2 * pairs:2].set(taker + shifted)
    return lengths[jax.random.permutation(jax.random.fold_in(stream_key, 2), count)]


def scatter_about(own_key, extent, deviation, reach, pieces=(), kind=jnp.bfloat16):
    drawn = deviation * jax.random.normal(own_key, extent, jnp.float32)
    if pieces:
        drawn = drawn * shard_levels(own_key, extent, pieces, -0.22, 0.18)
    return jnp.clip(drawn, -reach, reach).astype(kind)


def setup_inputs(seed: int = 0) -> dict:
    seeds = jax.random.split(jax.random.key(seed), 10)
    return {
        "displacement": scatter_about(seeds[0], (GRAINS, 3, NODES), 0.02, 0.1, ((0, 32),), jnp.float32),
        "velocity": scatter_about(seeds[1], (GRAINS, 3, NODES), 1.0, 6.0, ((0, 32),), jnp.float32),
        "centers": jnp.clip(jax.random.uniform(seeds[2], (3, GRAINS), jnp.float32, -4.0, 4.0) * shard_levels(seeds[2], (3, GRAINS), ((1, 32),), -0.4, 0.0), -4.0, 4.0),
        "tile_list": touch_ends(jax.random.randint(seeds[3], (GRAINS, TILES_G, 2), 0, NODES // BLK), jax.random.fold_in(seeds[3], 1), 0, (NODES // BLK) - 1).astype(jnp.int32),
        "broken_bits": draw_broken_bits(jax.random.fold_in(seeds[9], 71), 0),
        "surface_nodes": draw_surface_nodes(jax.random.fold_in(seeds[9], 71), 0),
        "send_order": jax.vmap(lambda own: jax.random.permutation(own, SBLK_DEV))(jax.random.split(seeds[6], OWNERS)).reshape((OWNERS, SBLK_DEV)).astype(jnp.int32),
        "pair_list": touch_ends(jax.random.randint(seeds[7], (OWNERS, PAIRS_DEV, 2), 0, SBLK_DEV), jax.random.fold_in(seeds[7], 1), 0, SBLK_DEV - 1).astype(jnp.int32),
        "pair_count": ragged_sizes(seeds[8], OWNERS, OWNERS * PAIRS_DEV // 2, PAIRS_DEV, 2).astype(jnp.int32),
    }


HORIZON = 3.0
BOND_STIFF = 5.0
CONTACT_STIFF = 0.02
CONTACT_DAMP = 0.05
CONTACT_RANGE = 9.0
TIME_STEP = 0.5

def lattice(node_count):
    node_index = jnp.arange(node_count, dtype=jnp.int32)
    return jnp.stack([node_index % 8, node_index // 8 % 8, node_index // 64]).astype(jnp.float32)

def unpack(bit_words):
    shifts = jnp.arange(8, dtype=jnp.int32)
    bit_table = jnp.right_shift(bit_words[:, None], shifts[None, :]) & 1
    return bit_table.reshape(BLK, BLK)

def bond_tile(rest_grid, now_grid, tile_pair, tile_words):
    row_start = tile_pair[0] * BLK
    col_start = tile_pair[1] * BLK
    rest_rows = lax.dynamic_slice_in_dim(rest_grid, row_start, BLK, 1)
    rest_cols = lax.dynamic_slice_in_dim(rest_grid, col_start, BLK, 1)
    now_rows = lax.dynamic_slice_in_dim(now_grid, row_start, BLK, 1)
    now_cols = lax.dynamic_slice_in_dim(now_grid, col_start, BLK, 1)
    rest_gap = rest_cols[:, None, :] - rest_rows[:, :, None]
    rest_len = jnp.sqrt(lax.optimization_barrier(jnp.sum(rest_gap * rest_gap, axis=0)))
    now_gap = now_cols[:, None, :] - now_rows[:, :, None]
    now_len = jnp.sqrt(lax.optimization_barrier(jnp.sum(now_gap * now_gap, axis=0)))
    live_bond = (rest_len > 0.5) & (rest_len <= HORIZON) & (unpack(tile_words) == 0)
    safe_rest = jnp.where(live_bond, rest_len, 1.0)
    safe_now = jnp.where(live_bond, now_len, 1.0)
    coefficient = jnp.where(live_bond, BOND_STIFF * (now_len - rest_len) / (safe_rest * safe_now), 0.0)
    return lax.optimization_barrier(jnp.sum(coefficient[None] * now_gap, axis=2))

def grain_bonds(displacement, tile_list, bit_words):
    rest_grid = lattice(displacement.shape[1])
    now_grid = rest_grid + displacement

    def tile_step(force_sum, entry_item):
        tile_pair, tile_words = entry_item
        tile_force = bond_tile(rest_grid, now_grid, tile_pair, tile_words)
        row_start = tile_pair[0] * BLK
        old_rows = lax.dynamic_slice_in_dim(force_sum, row_start, BLK, 1)
        return (lax.dynamic_update_slice_in_dim(force_sum, old_rows + tile_force, row_start, 1), None)
    force_sum, _ = lax.scan(tile_step, jnp.zeros_like(displacement), (tile_list, bit_words))
    return force_sum

def bonds_all(displacement, tile_list, bit_words):
    grains = displacement.shape[0]

    def grouped(array):
        return array.reshape((grains // 16, 16) + array.shape[1:])

    def group_step(entry_item):
        return jax.vmap(grain_bonds)(*entry_item)
    forces = lax.map(group_step, (grouped(displacement), grouped(tile_list), grouped(bit_words)))
    return forces.reshape(displacement.shape)

def contact_pair(left_block, right_block):
    gap_vec = left_block[:3, :, None] - right_block[:3, None, :]
    slip_vec = left_block[3:, :, None] - right_block[3:, None, :]
    weights = jnp.exp(-lax.optimization_barrier(jnp.sum(gap_vec * gap_vec, axis=0)) / CONTACT_RANGE)
    push_term = weights[None] * (CONTACT_STIFF * gap_vec - CONTACT_DAMP * slip_vec)
    return (lax.optimization_barrier(jnp.sum(push_term, axis=2)), -lax.optimization_barrier(jnp.sum(push_term, axis=1)))

def surface_blocks(displacement, velocity, centers, surface_nodes):
    rest_grid = lattice(displacement.shape[2])
    now_grid = rest_grid[None] + displacement + centers.T[:, :, None]
    full_state = jnp.concatenate([now_grid, velocity], axis=1)
    picked = jnp.take_along_axis(full_state, surface_nodes[:, None, :], axis=2)
    grains = picked.shape[0]
    return picked.reshape(grains, 6, SB, BLK).transpose(0, 2, 1, 3).reshape(grains * SB, 6, BLK)

def spread_surface(block_force, surface_nodes, node_count):
    grains = surface_nodes.shape[0]
    surface_force = block_force.reshape(grains, SB, 3, BLK).transpose(0, 2, 1, 3).reshape(grains, 3, SB * BLK)

    def one_grain(node_ids, node_force):
        return jnp.zeros((3, node_count), node_force.dtype).at[:, node_ids].add(node_force)
    return jax.vmap(one_grain)(surface_nodes, surface_force)

def reference(displacement, velocity, centers, tile_list, broken_bits, surface_nodes, send_order, pair_list, pair_count):
    bond_force = bonds_all(displacement, tile_list, broken_bits)
    blocks = surface_blocks(displacement, velocity, centers, surface_nodes)
    anchor = jnp.arange(OWNERS, dtype=jnp.int32)[:, None, None] * SBLK_DEV
    held_ids = (send_order.reshape(OWNERS, OWNERS, CAP) + anchor).transpose(1, 0, 2).reshape(OWNERS, SBLK_DEV)
    left_ids = jnp.take_along_axis(held_ids, pair_list[:, :, 0], axis=1)
    right_ids = jnp.take_along_axis(held_ids, pair_list[:, :, 1], axis=1)
    live_pairs = jnp.arange(PAIRS_DEV, dtype=jnp.int32)[None, :] < pair_count[:, None]

    def owner_step(accumulated, entry_item):
        left_one, right_one, in_range = entry_item
        left_force, right_force = jax.vmap(contact_pair)(blocks[left_one], blocks[right_one])
        live_mask = in_range.astype(left_force.dtype)[:, None, None]
        accumulated = accumulated.at[left_one].add(left_force * live_mask)
        accumulated = accumulated.at[right_one].add(right_force * live_mask)
        return (accumulated, None)
    start_force = jnp.zeros((blocks.shape[0], 3, BLK), blocks.dtype)
    block_force, _ = lax.scan(owner_step, start_force, (left_ids, right_ids, live_pairs))
    contact_force = spread_surface(block_force, surface_nodes, displacement.shape[2])
    force = bond_force + contact_force
    return (force, velocity + TIME_STEP * force)
```

```python
import functools
import math

import jax
import jax.numpy as jnp
from jax import lax
from jax.experimental import pallas as pl
from jax.experimental.pallas import tpu as pltpu
from jax.sharding import PartitionSpec as P

BLK = 128
HORIZON = 3.0
BOND_STIFF = 5.0
CONTACT_STIFF = 0.02
CONTACT_DAMP = 0.05
CONTACT_RANGE = 9.0
TIME_STEP = 0.5
VMEM_BYTES = 50 * 1024 * 1024
FAR = 100.0
BOND_UNROLL = 4
PAIR_UNROLL = 4
F32 = jnp.float32
BF16 = jnp.bfloat16


def iota(shape, axis):
    return lax.broadcasted_iota(jnp.int32, shape, axis)


def split3(value):
    one = value.astype(BF16).astype(F32)
    rest = value - one
    two = rest.astype(BF16).astype(F32)
    return one, two, (rest - two).astype(BF16).astype(F32)


def left_rows(value):
    one, two, three = split3(value)
    return jnp.concatenate([one, one, two, one, three, two], axis=0).astype(BF16)


def right_rows(value):
    one, two, three = split3(value)
    return jnp.concatenate([one, two, one, three, one, two], axis=0).astype(BF16)


def dot(left, right, left_dim, right_dim):
    return lax.dot_general(
        left, right, (((left_dim,), (right_dim,)), ((), ())), preferred_element_type=F32
    )


def split2(value):
    high = value.astype(BF16)
    return high, (value - high.astype(F32)).astype(BF16)


def stack_rows(pieces, width):
    row = iota((8, width), 0)
    total = jnp.zeros((8, width), F32)
    for number, piece in pieces.items():
        total = jnp.where(row == number, jnp.broadcast_to(piece, (8, width)), total)
    return total


def lattice_row(node):
    return (
        (node % 8).astype(F32) - 3.5,
        (node // 8 % 8).astype(F32) - 3.5,
        (node // 64).astype(F32) - 5.5,
    )


def pick_kernel(order, shift, velocity, centers, nodes, out, held):
    _, grains, count = shift.shape
    surface = nodes.shape[1]
    blocks = surface // BLK
    owners = out.shape[0]
    share = out.shape[1] // 6
    scale = math.sqrt(2.0 * math.log2(math.e) / CONTACT_RANGE)
    same = iota((grains, grains), 0) == iota((grains, grains), 1)
    offsets = [
        jnp.sum(jnp.where(same, centers[c : c + 1, :], 0.0), axis=1, keepdims=True)
        for c in range(3)
    ]
    for group in range(grains // 8):
        rows = slice(group * 8, group * 8 + 8)
        places = []
        speeds = []
        for tile in range(count // BLK):
            span = slice(tile * BLK, tile * BLK + BLK)
            rest = lattice_row(iota((8, BLK), 1) + tile * BLK)
            now = [rest[c] + shift[c, rows, span] + offsets[c][rows] for c in range(3)]
            places.append([scale * now[c] for c in range(3)])
            speeds.append(
                [
                    CONTACT_STIFF * now[c] - CONTACT_DAMP * velocity[c, rows, span]
                    for c in range(3)
                ]
            )
        for k in range(blocks):
            index = nodes[rows, k * BLK : k * BLK + BLK]
            low = index & (BLK - 1)
            high = index >> 7
            for c in range(6):
                source = places if c < 3 else speeds
                total = jnp.zeros((8, BLK), F32)
                for tile in range(count // BLK):
                    found = jnp.take_along_axis(source[tile][c % 3], low, axis=1)
                    total = jnp.where(high == tile, found, total)
                base = (c * blocks + k) * grains + group * 8
                held[base : base + 8, :] = total

    def send(d, carry):
        for cc in range(share):
            j = order[0, d * share + cc]
            row = (j % blocks) * grains + j // blocks
            for c in range(6):
                out[d, cc * 6 + c : cc * 6 + c + 1, :] = held[
                    pl.ds(row + c * blocks * grains, 1), :
                ]
        return carry

    lax.fori_loop(0, owners, send, 0)


def bond_kernel(tiles, shift, bits, nodes, force, place, lefts, rights, sums, spots, total, radius, square, spread, live):
    _, grains, count = shift.shape
    tile_count = bits.shape[1]
    surface = nodes.shape[1]
    blocks = count // BLK

    q = iota((BLK, BLK), 0)
    p = iota((BLK, BLK), 1)
    flat = (q % 8 - p % 8) ** 2 + (q // 8 % 8 - p // 8 % 8) ** 2
    for delta in range(-2, 3):
        squared = (flat + (2 * delta + q // 64 - p // 64) ** 2).astype(F32)
        kept = (squared > 0.25) & (squared <= HORIZON * HORIZON)
        square[delta + 2] = jnp.where(kept, squared, FAR)
        radius[delta + 2] = jnp.where(kept, jnp.sqrt(squared), 10.0)
    spread[...] = jnp.where(iota((16, BLK), 1) % 16 == iota((16, BLK), 0), 1.0, 0.0).astype(BF16)

    rest = lattice_row(iota((1, count), 1))
    ones = jnp.ones((1, count), F32)

    def prepare(g, carry):
        moved = [shift[c, pl.ds(g, 1), :] for c in range(3)]
        own = sum(2.0 * rest[c] * moved[c] + moved[c] * moved[c] for c in range(3))
        now = [rest[c] + moved[c] for c in range(3)]
        left = stack_rows(
            {0: moved[0], 1: moved[1], 2: moved[2], 3: rest[0], 4: rest[1], 5: rest[2], 6: own, 7: ones},
            count,
        )
        right = stack_rows(
            {
                0: -2.0 * now[0],
                1: -2.0 * now[1],
                2: -2.0 * now[2],
                3: -2.0 * moved[0],
                4: -2.0 * moved[1],
                5: -2.0 * moved[2],
                6: ones,
                7: own,
            },
            count,
        )
        spot = stack_rows({0: now[0], 1: now[1], 2: now[2], 3: ones}, count)
        left_all = left_rows(left)
        right_all = right_rows(right)
        one, two, three = split3(spot)
        sum_all = jnp.concatenate([one, two, three, jnp.zeros_like(one)], axis=0).astype(BF16)
        for h in range(blocks):
            span = slice(h * BLK, h * BLK + BLK)
            at = g * blocks + h
            lefts[at] = left_all[:, span]
            rights[at] = right_all[:, span]
            sums[at, :, :BLK] = sum_all[:, span]
            sums[at, :, BLK:] = sum_all[:, span]
            spots[at] = spot[:, span]
            total[at] = jnp.zeros((8, BLK), F32)

        listed = nodes[pl.ds(g, 1), :]
        low = listed & (BLK - 1)
        high = listed >> 7
        position = iota((1, surface), 1)
        row = iota((8, surface), 0)
        hit = row == jnp.broadcast_to(high, (8, surface))
        first = jnp.where(hit, jnp.broadcast_to((position % BLK + 1).astype(F32), (8, surface)), 0.0)
        second = jnp.where(hit, jnp.broadcast_to((position // BLK).astype(F32), (8, surface)), 0.0)
        chosen = jnp.concatenate([first, second], axis=0).astype(BF16)
        match = jnp.where(
            iota((BLK, surface), 0) == jnp.broadcast_to(low, (BLK, surface)), 1.0, 0.0
        ).astype(BF16)
        found = dot(chosen, match, 1, 1)
        code = (found[:8] + float(BLK) * found[8:]).astype(jnp.int32)
        for h in range(blocks):
            place[pl.ds(h * grains + g, 1), :] = code[h : h + 1, :]
        return carry

    lax.fori_loop(0, grains, prepare, 0)

    def enlist(g, held):
        for t in range(tile_count):
            gap = tiles[2 * t + 1, g] - tiles[2 * t, g]
            live[held] = g * tile_count + t
            held = held + jnp.where((gap <= 2) & (gap >= -2), 1, 0)
        return held

    live_count = lax.fori_loop(0, grains, enlist, 0)
    own_group = (iota((8, BLK), 1) // 16) == iota((8, BLK), 0)
    flag = jnp.left_shift(1, iota((8, BLK), 0))

    def step(n, carry):
        results = []
        for u in range(BOND_UNROLL):
            number = n * BOND_UNROLL + u
            good = number < live_count
            entry = live[jnp.where(good, number, 0)]
            g = entry // tile_count
            t = entry % tile_count
            a = tiles[2 * t, g]
            b = tiles[2 * t + 1, g]
            row_at = g * blocks + a
            col_at = g * blocks + b
            delta = b - a + 2
            excess = dot(lefts[col_at], rights[row_at], 0, 0)
            words = bits[g, pl.ds(t, 1), :].astype(F32)
            sorted_words = jnp.concatenate(
                [
                    jnp.where(
                        own_group,
                        jnp.broadcast_to(words[:, w * BLK : w * BLK + BLK], (8, BLK)),
                        0.0,
                    )
                    for w in range(16)
                ],
                axis=0,
            ).astype(BF16)
            turned = dot(spread[...], sorted_words, 1, 1).astype(jnp.int32)
            rest_square = square[delta]
            now_square = rest_square + excess
            inverse = lax.rsqrt(now_square)
            under = radius[delta] * (now_square * inverse) + rest_square
            bond = excess * inverse / under
            broken = jnp.concatenate(
                [jnp.broadcast_to(turned[w : w + 1], (8, BLK)) & flag for w in range(16)], axis=0
            )
            bond = jnp.where((broken == 0) & (rest_square < 0.5 * FAR), bond, 0.0)
            high, low = split2(bond)
            found = dot(sums[col_at], jnp.concatenate([high, low], axis=0), 1, 0)
            found = found[:8] + found[8:16] + found[16:24]
            gain = BOND_STIFF * (found - spots[row_at] * found[3:4])
            results.append((row_at, jnp.where(good, gain, 0.0)))
        for row_at, gain in results:
            total[row_at] = total[row_at] + gain
        return carry

    lax.fori_loop(0, (live_count + BOND_UNROLL - 1) // BOND_UNROLL, step, 0)

    def finish(g, carry):
        for h in range(blocks):
            for c in range(3):
                force[pl.ds((c * blocks + h) * grains + g, 1), :] = total[g * blocks + h, c : c + 1, :]
        return carry

    lax.fori_loop(0, grains, finish, 0)


def contact_kernel(pairs, count, received, out, lefts, rights, sums, total):
    owners = received.shape[0]
    share = received.shape[1] // 6

    def prepare(s, carry):
        for cc in range(share):
            at = s * share + cc
            line = [received[s, cc * 6 + c : cc * 6 + c + 1, :] for c in range(6)]
            own = -0.5 * (line[0] * line[0] + line[1] * line[1] + line[2] * line[2])
            one = jnp.ones((1, BLK), F32)
            base = {0: line[0], 1: line[1], 2: line[2]}
            lefts[at] = left_rows(stack_rows({**base, 3: own, 4: one}, BLK))
            rights[at] = right_rows(stack_rows({**base, 3: one, 4: own}, BLK))
            first, second, _ = split3(stack_rows({0: line[3], 1: line[4], 2: line[5], 3: one}, BLK))
            both = jnp.concatenate([first, second], axis=0).astype(BF16)
            sums[at, :, :BLK] = both
            sums[at, :, BLK:] = both
            total[at] = jnp.zeros((8, BLK), F32)
        return carry

    lax.fori_loop(0, owners, prepare, 0)
    live = count[0]

    def step(n, carry):
        results = []
        for u in range(PAIR_UNROLL):
            number = n * PAIR_UNROLL + u
            good = number < live
            at = jnp.where(good, number, 0)
            i = pairs[0, at]
            j = pairs[1, at]
            weight = jnp.exp2(dot(lefts[j], rights[i], 0, 0))
            high, low = split2(weight)
            gain_i = dot(sums[j], jnp.concatenate([high, low], axis=0), 1, 0)
            gain_j = dot(sums[i], jnp.concatenate([high, low], axis=1), 1, 1)
            results.append((i, jnp.where(good, gain_i[:8] + gain_i[8:], 0.0)))
            results.append((j, jnp.where(good, gain_j[:8] + gain_j[8:], 0.0)))
        for at, gain in results:
            total[at] = total[at] + gain
        return carry

    lax.fori_loop(0, (live + PAIR_UNROLL - 1) // PAIR_UNROLL, step, 0)

    def finish(s, carry):
        for cc in range(share):
            found = total[s * share + cc]
            weight = found[3:4]
            for c in range(3):
                out[s, cc * 3 + c : cc * 3 + c + 1, :] = (
                    received[s, cc * 6 + 3 + c : cc * 6 + 4 + c, :] * weight - found[c : c + 1]
                )
        return carry

    lax.fori_loop(0, owners, finish, 0)


def finish_kernel(order, returned, place, bond, velocity, force, speed, held):
    _, grains, count = velocity.shape
    owners = returned.shape[0]
    node_blocks = count // BLK
    share = returned.shape[1] // 3
    blocks = held.shape[0] // (3 * grains)

    def accept(d, carry):
        for cc in range(share):
            j = order[0, d * share + cc]
            row = (j % blocks) * grains + j // blocks
            for c in range(3):
                held[pl.ds(row + c * blocks * grains, 1), :] = returned[
                    d, cc * 3 + c : cc * 3 + c + 1, :
                ]
        return carry

    lax.fori_loop(0, owners, accept, 0)
    for group in range(grains // 8):
        rows = slice(group * 8, group * 8 + 8)
        for tile in range(count // BLK):
            span = slice(tile * BLK, tile * BLK + BLK)
            base = tile * grains + group * 8
            code = place[base : base + 8, :]
            spot = code - 1
            low = spot & (BLK - 1)
            high = jnp.where(code == 0, -1, spot >> 7)
            for c in range(3):
                total = jnp.zeros((8, BLK), F32)
                for k in range(blocks):
                    at = (c * blocks + k) * grains + group * 8
                    found = jnp.take_along_axis(held[at : at + 8, :], low, axis=1)
                    total = jnp.where(high == k, found, total)
                near = (c * node_blocks + tile) * grains + group * 8
                total = bond[near : near + 8, :] + total
                force[c, rows, span] = total
                speed[c, rows, span] = velocity[c, rows, span] + TIME_STEP * total


def on_device(displacement, velocity, centers, tile_list, broken_bits, surface_nodes, send_order, pair_list, pair_count):
    grains, _, count = displacement.shape
    owners = lax.axis_size("grain") * lax.axis_size("cell")
    slots = send_order.shape[1]
    share = slots // owners
    surface = surface_nodes.shape[1]
    blocks = surface // BLK
    node_blocks = count // BLK
    tile_count = tile_list.shape[1]
    shift = displacement.transpose(1, 0, 2)
    speed = velocity.transpose(1, 0, 2)
    tiles = tile_list.transpose(1, 2, 0).reshape(2 * tile_count, grains)
    pairs = pair_list[0].T
    vmem = pl.BlockSpec(memory_space=pltpu.VMEM)
    smem = pl.BlockSpec(memory_space=pltpu.SMEM)
    params = pltpu.CompilerParams(vmem_limit_bytes=VMEM_BYTES)

    outgoing = pl.pallas_call(
        pick_kernel,
        out_shape=jax.ShapeDtypeStruct((owners, 6 * share, BLK), F32),
        in_specs=[smem, vmem, vmem, vmem, vmem],
        out_specs=vmem,
        scratch_shapes=[pltpu.VMEM((6 * slots, BLK), F32)],
        compiler_params=params,
        name="pick",
    )(send_order, shift, speed, centers, surface_nodes)

    received = lax.all_to_all(outgoing, ("grain", "cell"), split_axis=0, concat_axis=0, tiled=True)

    bond, place = pl.pallas_call(
        bond_kernel,
        out_shape=(
            jax.ShapeDtypeStruct((3 * node_blocks * grains, BLK), F32),
            jax.ShapeDtypeStruct((node_blocks * grains, BLK), jnp.int32),
        ),
        in_specs=[smem, vmem, vmem, vmem],
        out_specs=(vmem, vmem),
        scratch_shapes=[
            pltpu.VMEM((grains * node_blocks, 48, BLK), BF16),
            pltpu.VMEM((grains * node_blocks, 48, BLK), BF16),
            pltpu.VMEM((grains * node_blocks, 32, 2 * BLK), BF16),
            pltpu.VMEM((grains * node_blocks, 8, BLK), F32),
            pltpu.VMEM((grains * node_blocks, 8, BLK), F32),
            pltpu.VMEM((5, BLK, BLK), F32),
            pltpu.VMEM((5, BLK, BLK), F32),
            pltpu.VMEM((16, BLK), BF16),
            pltpu.SMEM((grains * tile_count + 1,), jnp.int32),
        ],
        compiler_params=params,
        cost_estimate=pl.CostEstimate(flops=4_000_000_000, bytes_accessed=3_000_000, transcendentals=4_000_000),
        name="bond",
    )(tiles, shift, broken_bits, surface_nodes)

    slot_force = pl.pallas_call(
        contact_kernel,
        out_shape=jax.ShapeDtypeStruct((owners, 3 * share, BLK), F32),
        in_specs=[smem, smem, vmem],
        out_specs=vmem,
        scratch_shapes=[
            pltpu.VMEM((slots, 48, BLK), BF16),
            pltpu.VMEM((slots, 48, BLK), BF16),
            pltpu.VMEM((slots, 16, 2 * BLK), BF16),
            pltpu.VMEM((slots, 8, BLK), F32),
        ],
        compiler_params=params,
        name="contact",
    )(pairs, pair_count, received)

    returned = lax.all_to_all(slot_force, ("grain", "cell"), split_axis=0, concat_axis=0, tiled=True)

    force, new_speed = pl.pallas_call(
        finish_kernel,
        out_shape=(jax.ShapeDtypeStruct((3, grains, count), F32),) * 2,
        in_specs=[smem, vmem, vmem, vmem, vmem],
        out_specs=(vmem, vmem),
        scratch_shapes=[pltpu.VMEM((3 * slots, BLK), F32)],
        compiler_params=params,
        name="finish",
    )(send_order, returned, place, bond, speed)
    return force.transpose(1, 0, 2), new_speed.transpose(1, 0, 2)


def solution(mesh):
    own = ("grain", "cell")
    return jax.shard_map(
        on_device,
        mesh=mesh,
        in_specs=(
            P(own, None, None),
            P(own, None, None),
            P(None, own),
            P(own, None, None),
            P(own, None, None),
            P(own, None),
            P(own, None),
            P(own, None, None),
            P(own),
        ),
        out_specs=(P(own, None, None), P(own, None, None)),
        check_vma=False,
    )
```

```python
import functools
import math

import jax
import jax.numpy as jnp
from jax import lax
from jax.experimental import pallas as pl
from jax.experimental.pallas import tpu as pltpu
from jax.sharding import PartitionSpec as P

BLK = 128
HORIZON = 3.0
BOND_STIFF = 5.0
CONTACT_STIFF = 0.02
CONTACT_DAMP = 0.05
CONTACT_RANGE = 9.0
TIME_STEP = 0.5
VMEM_BYTES = 32 * 1024 * 1024
FAR = 100.0
BOND_UNROLL = 4
PAIR_UNROLL = 8
GRAIN_UNROLL = 4
OWNER_UNROLL = 2
FIRST_SHARE = 5
ALL_SHARES = 8
F32 = jnp.float32
BF16 = jnp.bfloat16


def iota(shape, axis):
    return lax.broadcasted_iota(jnp.int32, shape, axis)


def split3(value):
    one = value.astype(BF16).astype(F32)
    rest = value - one
    two = rest.astype(BF16).astype(F32)
    return one, two, (rest - two).astype(BF16).astype(F32)


def left_rows(value):
    one, two, three = split3(value)
    return jnp.concatenate([one, one, two, one, three, two], axis=0).astype(BF16)


def right_rows(value):
    one, two, three = split3(value)
    return jnp.concatenate([one, two, one, three, one, two], axis=0).astype(BF16)


def dot(left, right, left_dim, right_dim):
    return lax.dot_general(
        left, right, (((left_dim,), (right_dim,)), ((), ())), preferred_element_type=F32
    )


def split2(value):
    high = value.astype(BF16)
    return high, (value - high.astype(F32)).astype(BF16)


def stack_rows(pieces, width):
    row = iota((8, width), 0)
    total = jnp.zeros((8, width), F32)
    for number, piece in pieces.items():
        total = jnp.where(row == number, jnp.broadcast_to(piece, (8, width)), total)
    return total


def lattice_row(node):
    return (
        (node % 8).astype(F32) - 3.5,
        (node // 8 % 8).astype(F32) - 3.5,
        (node // 64).astype(F32) - 5.5,
    )


def pick_kernel(order, shift_in, velocity_in, centers, nodes_in, out, held, shift, velocity, nodes, arrived):
    copies = [
        pltpu.make_async_copy(source, target, arrived.at[number])
        for number, (source, target) in enumerate(
            ((shift_in, shift), (velocity_in, velocity), (nodes_in, nodes))
        )
    ]
    for copy in copies:
        copy.start()
    _, grains, count = shift.shape
    surface = nodes.shape[1]
    blocks = surface // BLK
    owners = out.shape[0]
    share = out.shape[1] // 6
    scale = math.sqrt(2.0 * math.log2(math.e) / CONTACT_RANGE)
    same = iota((grains, grains), 0) == iota((grains, grains), 1)
    offsets = [
        jnp.sum(jnp.where(same, centers[c : c + 1, :], 0.0), axis=1, keepdims=True)
        for c in range(3)
    ]
    for copy in copies:
        copy.wait()
    for group in range(grains // 8):
        rows = slice(group * 8, group * 8 + 8)
        places = []
        speeds = []
        for tile in range(count // BLK):
            span = slice(tile * BLK, tile * BLK + BLK)
            rest = lattice_row(iota((8, BLK), 1) + tile * BLK)
            now = [rest[c] + shift[c, rows, span] + offsets[c][rows] for c in range(3)]
            places.append([scale * now[c] for c in range(3)])
            speeds.append(
                [
                    CONTACT_STIFF * now[c] - CONTACT_DAMP * velocity[c, rows, span]
                    for c in range(3)
                ]
            )
        for k in range(blocks):
            index = nodes[rows, k * BLK : k * BLK + BLK]
            low = index & (BLK - 1)
            high = index >> 7
            for c in range(6):
                source = places if c < 3 else speeds
                total = jnp.zeros((8, BLK), F32)
                for tile in range(count // BLK):
                    found = jnp.take_along_axis(source[tile][c % 3], low, axis=1)
                    total = jnp.where(high == tile, found, total)
                base = (c * blocks + k) * grains + group * 8
                held[base : base + 8, :] = total

    def send(d, carry):
        for cc in range(share):
            j = order[0, d * share + cc]
            row = (j % blocks) * grains + j // blocks
            for c in range(6):
                out[d, cc * 6 + c : cc * 6 + c + 1, :] = held[
                    pl.ds(row + c * blocks * grains, 1), :
                ]
        return carry

    lax.fori_loop(0, owners, send, 0)


def bond_kernel(first, grains, tiles, shift, bits, nodes, force, place, lefts, rights, sums, spots, total, radius, square, spread, live):
    count = shift.shape[2]
    tile_count = bits.shape[1]
    surface = nodes.shape[1]
    blocks = count // BLK

    q = iota((BLK, BLK), 0)
    p = iota((BLK, BLK), 1)
    flat = (q % 8 - p % 8) ** 2 + (q // 8 % 8 - p // 8 % 8) ** 2
    for delta in range(-2, 3):
        squared = (flat + (2 * delta + q // 64 - p // 64) ** 2).astype(F32)
        kept = (squared > 0.25) & (squared <= HORIZON * HORIZON)
        square[delta + 2] = jnp.where(kept, squared, FAR)
        radius[delta + 2] = jnp.where(kept, jnp.sqrt(squared), 10.0)
    spread[...] = jnp.where(iota((16, BLK), 1) % 16 == iota((16, BLK), 0), 1.0, 0.0).astype(BF16)

    rest = lattice_row(iota((1, count), 1))
    ones = jnp.ones((1, count), F32)

    def prepare_one(g):
        moved = [shift[c, pl.ds(first + g, 1), :] for c in range(3)]
        own = sum(2.0 * rest[c] * moved[c] + moved[c] * moved[c] for c in range(3))
        now = [rest[c] + moved[c] for c in range(3)]
        left = stack_rows(
            {0: moved[0], 1: moved[1], 2: moved[2], 3: rest[0], 4: rest[1], 5: rest[2], 6: own, 7: ones},
            count,
        )
        right = stack_rows(
            {
                0: -2.0 * now[0],
                1: -2.0 * now[1],
                2: -2.0 * now[2],
                3: -2.0 * moved[0],
                4: -2.0 * moved[1],
                5: -2.0 * moved[2],
                6: ones,
                7: own,
            },
            count,
        )
        spot = stack_rows({0: now[0], 1: now[1], 2: now[2], 3: ones}, count)
        left_all = left_rows(left)
        right_all = right_rows(right)
        one, two, three = split3(spot)
        sum_all = jnp.concatenate([one, two, three, jnp.zeros_like(one)], axis=0).astype(BF16)
        listed = nodes[pl.ds(first + g, 1), :]
        low = listed & (BLK - 1)
        high = listed >> 7
        position = iota((1, surface), 1)
        row = iota((8, surface), 0)
        hit = row == jnp.broadcast_to(high, (8, surface))
        within = jnp.where(hit, jnp.broadcast_to((position % BLK + 1).astype(F32), (8, surface)), 0.0)
        group = jnp.where(hit, jnp.broadcast_to((position // BLK).astype(F32), (8, surface)), 0.0)
        chosen = jnp.concatenate([within, group], axis=0).astype(BF16)
        match = jnp.where(
            iota((BLK, surface), 0) == jnp.broadcast_to(low, (BLK, surface)), 1.0, 0.0
        ).astype(BF16)
        found = dot(chosen, match, 1, 1)
        code = (found[:8] + float(BLK) * found[8:]).astype(jnp.int32)
        return left_all, right_all, sum_all, spot, code

    def prepare(n, carry):
        ready = [(n * GRAIN_UNROLL + u, prepare_one(n * GRAIN_UNROLL + u)) for u in range(GRAIN_UNROLL)]
        for g, (left_all, right_all, sum_all, spot, code) in ready:
            for h in range(blocks):
                span = slice(h * BLK, h * BLK + BLK)
                at = g * blocks + h
                lefts[at] = left_all[:, span]
                rights[at] = right_all[:, span]
                sums[at, :, :BLK] = sum_all[:, span]
                sums[at, :, BLK:] = sum_all[:, span]
                spots[at] = spot[:, span]
                total[at] = jnp.zeros((8, BLK), F32)
                place[pl.ds(h * grains + g, 1), :] = code[h : h + 1, :]
        return carry

    lax.fori_loop(0, grains // GRAIN_UNROLL, prepare, 0)

    def enlist(g, held):
        for t in range(tile_count):
            gap = tiles[2 * t + 1, first + g] - tiles[2 * t, first + g]
            live[held] = g * tile_count + t
            held = held + jnp.where((gap <= 2) & (gap >= -2), 1, 0)
        return held

    live_count = lax.fori_loop(0, grains, enlist, 0)
    own_group = (iota((8, BLK), 1) // 16) == iota((8, BLK), 0)
    flag = jnp.left_shift(1, iota((8, BLK), 0))

    def step(n, carry):
        results = []
        for u in range(BOND_UNROLL):
            number = n * BOND_UNROLL + u
            good = number < live_count
            entry = live[jnp.where(good, number, 0)]
            g = entry // tile_count
            t = entry % tile_count
            a = tiles[2 * t, first + g]
            b = tiles[2 * t + 1, first + g]
            row_at = g * blocks + a
            col_at = g * blocks + b
            delta = b - a + 2
            excess = dot(lefts[col_at], rights[row_at], 0, 0)
            words = bits[first + g, pl.ds(t, 1), :].astype(F32)
            sorted_words = jnp.concatenate(
                [
                    jnp.where(
                        own_group,
                        jnp.broadcast_to(words[:, w * BLK : w * BLK + BLK], (8, BLK)),
                        0.0,
                    )
                    for w in range(16)
                ],
                axis=0,
            ).astype(BF16)
            turned = dot(spread[...], sorted_words, 1, 1).astype(jnp.int32)
            rest_square = square[delta]
            now_square = rest_square + excess
            inverse = lax.rsqrt(now_square)
            under = radius[delta] * (now_square * inverse) + rest_square
            bond = excess * inverse / under
            broken = jnp.concatenate(
                [jnp.broadcast_to(turned[w : w + 1], (8, BLK)) & flag for w in range(16)], axis=0
            )
            bond = jnp.where((broken == 0) & (rest_square < 0.5 * FAR), bond, 0.0)
            high, low = split2(bond)
            found = dot(sums[col_at], jnp.concatenate([high, low], axis=0), 1, 0)
            found = found[:8] + found[8:16] + found[16:24]
            gain = BOND_STIFF * (found - spots[row_at] * found[3:4])
            results.append((row_at, jnp.where(good, gain, 0.0)))
        for row_at, gain in results:
            total[row_at] = total[row_at] + gain
        return carry

    lax.fori_loop(0, (live_count + BOND_UNROLL - 1) // BOND_UNROLL, step, 0)

    def finish(g, carry):
        for h in range(blocks):
            for c in range(3):
                force[pl.ds((c * blocks + h) * grains + g, 1), :] = total[g * blocks + h, c : c + 1, :]
        return carry

    lax.fori_loop(0, grains, finish, 0)


def contact_kernel(pairs, count, received, out, lefts, rights, sums, total):
    owners = received.shape[0]
    share = received.shape[1] // 6

    def prepare(n, carry):
        for u in range(OWNER_UNROLL * share):
            at = n * OWNER_UNROLL * share + u
            s = n * OWNER_UNROLL + u // share
            cc = u % share
            line = [received[s, cc * 6 + c : cc * 6 + c + 1, :] for c in range(6)]
            own = -0.5 * (line[0] * line[0] + line[1] * line[1] + line[2] * line[2])
            one = jnp.ones((1, BLK), F32)
            base = {0: line[0], 1: line[1], 2: line[2]}
            lefts[at] = left_rows(stack_rows({**base, 3: own, 4: one}, BLK))
            rights[at] = right_rows(stack_rows({**base, 3: one, 4: own}, BLK))
            first, second, _ = split3(stack_rows({0: line[3], 1: line[4], 2: line[5], 3: one}, BLK))
            both = jnp.concatenate([first, second], axis=0).astype(BF16)
            sums[at, :, :BLK] = both
            sums[at, :, BLK:] = both
            total[at] = jnp.zeros((8, BLK), F32)
        return carry

    lax.fori_loop(0, owners // OWNER_UNROLL, prepare, 0)
    live = count[0]

    def step(n, carry):
        results = []
        for u in range(PAIR_UNROLL):
            number = n * PAIR_UNROLL + u
            good = number < live
            at = jnp.where(good, number, 0)
            i = pairs[0, at]
            j = pairs[1, at]
            weight = jnp.exp2(dot(lefts[j], rights[i], 0, 0))
            high, low = split2(weight)
            gain_i = dot(sums[j], jnp.concatenate([high, low], axis=0), 1, 0)
            gain_j = dot(sums[i], jnp.concatenate([high, low], axis=1), 1, 1)
            results.append((i, jnp.where(good, gain_i[:8] + gain_i[8:], 0.0)))
            results.append((j, jnp.where(good, gain_j[:8] + gain_j[8:], 0.0)))
        for at, gain in results:
            total[at] = total[at] + gain
        return carry

    lax.fori_loop(0, (live + PAIR_UNROLL - 1) // PAIR_UNROLL, step, 0)

    def finish(s, carry):
        for cc in range(share):
            found = total[s * share + cc]
            weight = found[3:4]
            for c in range(3):
                out[s, cc * 3 + c : cc * 3 + c + 1, :] = (
                    received[s, cc * 6 + 3 + c : cc * 6 + 4 + c, :] * weight - found[c : c + 1]
                )
        return carry

    lax.fori_loop(0, owners, finish, 0)


def finish_kernel(cut, order, returned, place_a, bond_a, place_b, bond_b, velocity, force, speed, held):
    _, grains, count = velocity.shape
    owners = returned.shape[0]
    node_blocks = count // BLK
    share = returned.shape[1] // 3
    blocks = held.shape[0] // (3 * grains)

    def accept(d, carry):
        for cc in range(share):
            j = order[0, d * share + cc]
            row = (j % blocks) * grains + j // blocks
            for c in range(3):
                held[pl.ds(row + c * blocks * grains, 1), :] = returned[
                    d, cc * 3 + c : cc * 3 + c + 1, :
                ]
        return carry

    lax.fori_loop(0, owners, accept, 0)
    for group in range(grains // 8):
        rows = slice(group * 8, group * 8 + 8)
        for tile in range(count // BLK):
            span = slice(tile * BLK, tile * BLK + BLK)
            early = group * 8 < cut
            place, bond = (place_a, bond_a) if early else (place_b, bond_b)
            part = cut if early else grains - cut
            own = group * 8 - (0 if early else cut)
            base = tile * part + own
            code = place[base : base + 8, :]
            spot = code - 1
            low = spot & (BLK - 1)
            high = jnp.where(code == 0, -1, spot >> 7)
            for c in range(3):
                total = jnp.zeros((8, BLK), F32)
                for k in range(blocks):
                    at = (c * blocks + k) * grains + group * 8
                    found = jnp.take_along_axis(held[at : at + 8, :], low, axis=1)
                    total = jnp.where(high == k, found, total)
                near = (c * node_blocks + tile) * part + own
                total = bond[near : near + 8, :] + total
                force[c, rows, span] = total
                speed[c, rows, span] = velocity[c, rows, span] + TIME_STEP * total


def on_device(displacement, velocity, centers, tile_list, broken_bits, surface_nodes, send_order, pair_list, pair_count):
    grains, _, count = displacement.shape
    owners = lax.axis_size("grain") * lax.axis_size("cell")
    slots = send_order.shape[1]
    share = slots // owners
    surface = surface_nodes.shape[1]
    blocks = surface // BLK
    node_blocks = count // BLK
    tile_count = tile_list.shape[1]
    shift = displacement.transpose(1, 0, 2)
    speed = velocity.transpose(1, 0, 2)
    tiles = tile_list.transpose(1, 2, 0).reshape(2 * tile_count, grains)
    pairs = pair_list[0].T
    vmem = pl.BlockSpec(memory_space=pltpu.VMEM)
    smem = pl.BlockSpec(memory_space=pltpu.SMEM)
    hbm = pl.BlockSpec(memory_space=pltpu.HBM)
    params = pltpu.CompilerParams(vmem_limit_bytes=VMEM_BYTES)

    outgoing = pl.pallas_call(
        pick_kernel,
        out_shape=jax.ShapeDtypeStruct((owners, 6 * share, BLK), F32),
        in_specs=[smem, hbm, hbm, vmem, hbm],
        out_specs=vmem,
        scratch_shapes=[
            pltpu.VMEM((6 * slots, BLK), F32),
            pltpu.VMEM((3, grains, count), F32),
            pltpu.VMEM((3, grains, count), F32),
            pltpu.VMEM((grains, surface), jnp.int32),
            pltpu.SemaphoreType.DMA((3,)),
        ],
        compiler_params=params,
        name="pick",
    )(send_order, shift, speed, centers, surface_nodes)

    def bonds(first, part, shift_now):
        return pl.pallas_call(
            functools.partial(bond_kernel, first, part),
            out_shape=(
                jax.ShapeDtypeStruct((3 * node_blocks * part, BLK), F32),
                jax.ShapeDtypeStruct((node_blocks * part, BLK), jnp.int32),
            ),
            in_specs=[smem, vmem, vmem, vmem],
            out_specs=(vmem, vmem),
            scratch_shapes=[
                pltpu.VMEM((part * node_blocks, 48, BLK), BF16),
                pltpu.VMEM((part * node_blocks, 48, BLK), BF16),
                pltpu.VMEM((part * node_blocks, 32, 2 * BLK), BF16),
                pltpu.VMEM((part * node_blocks, 8, BLK), F32),
                pltpu.VMEM((part * node_blocks, 8, BLK), F32),
                pltpu.VMEM((5, BLK, BLK), F32),
                pltpu.VMEM((5, BLK, BLK), F32),
                pltpu.VMEM((16, BLK), BF16),
                pltpu.SMEM((part * tile_count + 1,), jnp.int32),
            ],
            compiler_params=params,
            cost_estimate=pl.CostEstimate(
                flops=4_000_000_000, bytes_accessed=3_000_000, transcendentals=4_000_000
            ),
            name="bond",
        )(tiles, shift_now, broken_bits, surface_nodes)

    cut = grains * FIRST_SHARE // ALL_SHARES // 8 * 8
    outgoing, shift_now = lax.optimization_barrier((outgoing, shift))
    received = lax.all_to_all(outgoing, ("grain", "cell"), split_axis=0, concat_axis=0, tiled=True)
    bond_a, place_a = bonds(0, cut, shift_now)
    received, bond_a, place_a = lax.optimization_barrier((received, bond_a, place_a))

    slot_force = pl.pallas_call(
        contact_kernel,
        out_shape=jax.ShapeDtypeStruct((owners, 3 * share, BLK), F32),
        in_specs=[smem, smem, vmem],
        out_specs=vmem,
        scratch_shapes=[
            pltpu.VMEM((slots, 48, BLK), BF16),
            pltpu.VMEM((slots, 48, BLK), BF16),
            pltpu.VMEM((slots, 16, 2 * BLK), BF16),
            pltpu.VMEM((slots, 8, BLK), F32),
        ],
        compiler_params=params,
        name="contact",
    )(pairs, pair_count, received)

    slot_force, shift_now = lax.optimization_barrier((slot_force, shift_now))
    returned = lax.all_to_all(slot_force, ("grain", "cell"), split_axis=0, concat_axis=0, tiled=True)
    bond_b, place_b = bonds(cut, grains - cut, shift_now)

    force, new_speed = pl.pallas_call(
        functools.partial(finish_kernel, cut),
        out_shape=(jax.ShapeDtypeStruct((3, grains, count), F32),) * 2,
        in_specs=[smem, vmem, vmem, vmem, vmem, vmem, vmem],
        out_specs=(vmem, vmem),
        scratch_shapes=[pltpu.VMEM((3 * slots, BLK), F32)],
        compiler_params=params,
        name="finish",
    )(send_order, returned, place_a, bond_a, place_b, bond_b, speed)
    return force.transpose(1, 0, 2), new_speed.transpose(1, 0, 2)


def solution(mesh):
    own = ("grain", "cell")
    return jax.shard_map(
        on_device,
        mesh=mesh,
        in_specs=(
            P(own, None, None),
            P(own, None, None),
            P(None, own),
            P(own, None, None),
            P(own, None, None),
            P(own, None),
            P(own, None),
            P(own, None, None),
            P(own),
        ),
        out_specs=(P(own, None, None), P(own, None, None)),
        check_vma=False,
    )
```

```python
import functools
import math

import jax
import jax.numpy as jnp
from jax import lax
from jax.experimental import pallas as pl
from jax.experimental.pallas import tpu as pltpu
from jax.sharding import PartitionSpec as P

BLK = 128
HORIZON = 3.0
BOND_STIFF = 5.0
CONTACT_STIFF = 0.02
CONTACT_DAMP = 0.05
CONTACT_RANGE = 9.0
TIME_STEP = 0.5
VMEM_BYTES = 32 * 1024 * 1024
PICK_BYTES = 60 * 1024 * 1024
FAR = 100.0
BOND_UNROLL = 8
FAR_UNROLL = 4
PAIR_UNROLL = 16
GRAIN_UNROLL = 4
OWNER_UNROLL = 2
FIRST_SHARE = 6
ALL_SHARES = 8
F32 = jnp.float32
BF16 = jnp.bfloat16


def iota(shape, axis):
    return lax.broadcasted_iota(jnp.int32, shape, axis)


def split3(value):
    one = value.astype(BF16).astype(F32)
    rest = value - one
    two = rest.astype(BF16).astype(F32)
    return one, two, (rest - two).astype(BF16).astype(F32)


def left_rows(value):
    one, two, three = split3(value)
    return jnp.concatenate([one, one, two, one, three, two], axis=0).astype(BF16)


def right_rows(value):
    one, two, three = split3(value)
    return jnp.concatenate([one, two, one, three, one, two], axis=0).astype(BF16)


def dot(left, right, left_dim, right_dim):
    return lax.dot_general(
        left, right, (((left_dim,), (right_dim,)), ((), ())), preferred_element_type=F32
    )


def split2(value):
    high = value.astype(BF16)
    return high, (value - high.astype(F32)).astype(BF16)


def stack_rows(pieces, width, kind=F32):
    row = iota((8, width), 0)
    total = jnp.zeros((8, width), kind)
    for number, piece in pieces.items():
        total = jnp.where(row == number, jnp.broadcast_to(piece, (8, width)), total)
    return total


def lattice_row(node):
    return (
        (node % 8).astype(F32) - 3.5,
        (node // 8 % 8).astype(F32) - 3.5,
        (node // 64).astype(F32) - 5.5,
    )


def pick_kernel(order, shift_in, velocity_in, centers, nodes_in, out, held, shift, velocity, nodes, arrived):
    copies = [
        pltpu.make_async_copy(source, target, arrived.at[number])
        for number, (source, target) in enumerate(
            ((shift_in, shift), (velocity_in, velocity), (nodes_in, nodes))
        )
    ]
    for copy in copies:
        copy.start()
    _, grains, count = shift.shape
    surface = nodes.shape[1]
    blocks = surface // BLK
    owners = out.shape[0]
    share = out.shape[1] // 6
    scale = math.sqrt(2.0 * math.log2(math.e) / CONTACT_RANGE)
    same = iota((grains, grains), 0) == iota((grains, grains), 1)
    offsets = [
        jnp.sum(jnp.where(same, centers[c : c + 1, :], 0.0), axis=1, keepdims=True)
        for c in range(3)
    ]
    for copy in copies:
        copy.wait()
    for group in range(grains // 8):
        rows = slice(group * 8, group * 8 + 8)
        places = []
        speeds = []
        for tile in range(count // BLK):
            span = slice(tile * BLK, tile * BLK + BLK)
            rest = lattice_row(iota((8, BLK), 1) + tile * BLK)
            now = [rest[c] + shift[c, rows, span] + offsets[c][rows] for c in range(3)]
            places.append([scale * now[c] for c in range(3)])
            speeds.append(
                [
                    CONTACT_STIFF * now[c] - CONTACT_DAMP * velocity[c, rows, span]
                    for c in range(3)
                ]
            )
        for k in range(blocks):
            index = nodes[rows, k * BLK : k * BLK + BLK]
            low = index & (BLK - 1)
            high = index >> 7
            for c in range(6):
                source = places if c < 3 else speeds
                total = jnp.zeros((8, BLK), F32)
                for tile in range(count // BLK):
                    found = jnp.take_along_axis(source[tile][c % 3], low, axis=1)
                    total = jnp.where(high == tile, found, total)
                base = (c * blocks + k) * grains + group * 8
                held[base : base + 8, :] = total

    def send(d, carry):
        for cc in range(share):
            j = order[0, d * share + cc]
            row = (j % blocks) * grains + j // blocks
            for c in range(6):
                out[d, cc * 6 + c : cc * 6 + c + 1, :] = held[
                    pl.ds(row + c * blocks * grains, 1), :
                ]
        return carry

    lax.fori_loop(0, owners, send, 0)


def bond_kernel(first, grains, tiles, shift, bits, nodes, force, place, lefts, rights, sums, spots, total, inverse, square, dead, spread, fold, near, far):
    count = shift.shape[2]
    tile_count = bits.shape[1]
    surface = nodes.shape[1]
    blocks = count // BLK

    q = iota((BLK, BLK), 0)
    p = iota((BLK, BLK), 1)
    flat = (q % 8 - p % 8) ** 2 + (q // 8 % 8 - p // 8 % 8) ** 2
    for delta in range(-1, 2):
        squared = (flat + (2 * delta + q // 64 - p // 64) ** 2).astype(F32)
        kept = (squared > 0.25) & (squared <= HORIZON * HORIZON)
        square[delta + 1] = jnp.where(kept, squared, FAR)
        inverse[delta + 1] = 1.0 / jnp.sqrt(jnp.where(kept, squared, FAR))
        dead[delta + 1] = jnp.where(kept, 0, 255)
    fold[...] = jnp.where(q // 16 == p % 8, 1.0, 0.0).astype(BF16)
    spread[...] = jnp.where(iota((16, BLK), 1) % 16 == iota((16, BLK), 0), 1.0, 0.0).astype(BF16)

    rest = lattice_row(iota((1, count), 1))
    ones = jnp.ones((1, count), F32)

    def prepare_one(g):
        moved = [shift[c, pl.ds(first + g, 1), :] for c in range(3)]
        own = sum(2.0 * rest[c] * moved[c] + moved[c] * moved[c] for c in range(3))
        now = [rest[c] + moved[c] for c in range(3)]
        left = stack_rows(
            {0: moved[0], 1: moved[1], 2: moved[2], 3: rest[0], 4: rest[1], 5: rest[2], 6: own, 7: ones},
            count,
        )
        right = stack_rows(
            {
                0: -2.0 * now[0],
                1: -2.0 * now[1],
                2: -2.0 * now[2],
                3: -2.0 * moved[0],
                4: -2.0 * moved[1],
                5: -2.0 * moved[2],
                6: ones,
                7: own,
            },
            count,
        )
        spot = stack_rows({0: now[0], 1: now[1], 2: now[2], 3: ones}, count)
        left_all = left_rows(left)
        right_all = right_rows(right)
        one, two, three = split3(spot)
        sum_all = jnp.concatenate([one, two, three, jnp.zeros_like(one)], axis=0).astype(BF16)
        listed = nodes[pl.ds(first + g, 1), :]
        low = listed & (BLK - 1)
        high = listed >> 7
        position = iota((1, surface), 1)
        row = iota((8, surface), 0)
        hit = row == jnp.broadcast_to(high, (8, surface))
        within = jnp.where(hit, jnp.broadcast_to((position % BLK + 1).astype(F32), (8, surface)), 0.0)
        group = jnp.where(hit, jnp.broadcast_to((position // BLK).astype(F32), (8, surface)), 0.0)
        chosen = jnp.concatenate([within, group], axis=0).astype(BF16)
        match = jnp.where(
            iota((BLK, surface), 0) == jnp.broadcast_to(low, (BLK, surface)), 1.0, 0.0
        ).astype(BF16)
        found = dot(chosen, match, 1, 1)
        code = (found[:8] + float(BLK) * found[8:]).astype(jnp.int32)
        return left_all, right_all, sum_all, spot, code

    def prepare(n, carry):
        ready = [(n * GRAIN_UNROLL + u, prepare_one(n * GRAIN_UNROLL + u)) for u in range(GRAIN_UNROLL)]
        for g, (left_all, right_all, sum_all, spot, code) in ready:
            for h in range(blocks):
                span = slice(h * BLK, h * BLK + BLK)
                at = g * blocks + h
                lefts[at] = left_all[:, span]
                rights[at] = right_all[:, span]
                sums[at, :, :BLK] = sum_all[:, span]
                sums[at, :, BLK:] = sum_all[:, span]
                spots[at] = spot[:, span]
                total[at] = jnp.zeros((8, BLK), F32)
                place[pl.ds(h * grains + g, 1), :] = code[h : h + 1, :]
        return carry

    lax.fori_loop(0, grains // GRAIN_UNROLL, prepare, 0)

    def enlist(g, carry):
        near_held, far_held = carry
        for t in range(tile_count):
            gap = tiles[2 * t + 1, first + g] - tiles[2 * t, first + g]
            near[near_held] = g * tile_count + t
            far[far_held] = g * tile_count + t
            near_held = near_held + jnp.where((gap <= 1) & (gap >= -1), 1, 0)
            far_held = far_held + jnp.where((gap == 2) | (gap == -2), 1, 0)
        return near_held, far_held

    near_count, far_count = lax.fori_loop(0, grains, enlist, (0, 0))
    own_group = (iota((8, BLK), 1) // 16) == iota((8, BLK), 0)
    flag_all = jnp.left_shift(1, iota((BLK, BLK), 0) % 8)

    def step(n, carry):
        results = []
        for u in range(BOND_UNROLL):
            number = n * BOND_UNROLL + u
            good = number < near_count
            entry = near[jnp.where(good, number, 0)]
            g = entry // tile_count
            t = entry % tile_count
            a = tiles[2 * t, first + g]
            b = tiles[2 * t + 1, first + g]
            row_at = g * blocks + a
            col_at = g * blocks + b
            delta = b - a + 1
            excess = dot(lefts[col_at], rights[row_at], 0, 0)
            words = bits[first + g, pl.ds(t, 1), :].astype(F32)
            sorted_words = jnp.concatenate(
                [
                    jnp.where(
                        own_group,
                        jnp.broadcast_to(words[:, w * BLK : w * BLK + BLK], (8, BLK)),
                        0.0,
                    )
                    for w in range(16)
                ],
                axis=0,
            ).astype(BF16)
            turned = dot(spread[...], sorted_words, 1, 1).astype(jnp.int32)
            bond = inverse[delta] - lax.rsqrt(square[delta] + excess)
            flags = jnp.concatenate(
                [jnp.broadcast_to(turned[w : w + 1], (8, BLK)) for w in range(16)], axis=0
            )
            bond = jnp.where(((flags | dead[delta]) & flag_all) == 0, bond, 0.0)
            high, low = split2(bond)
            found = dot(sums[col_at], jnp.concatenate([high, low], axis=0), 1, 0)
            found = found[:8] + found[8:16] + found[16:24]
            gain = BOND_STIFF * (found - spots[row_at] * found[3:4])
            results.append((row_at, jnp.where(good, gain, 0.0)))
        for row_at, gain in results:
            total[row_at] = total[row_at] + gain
        return carry

    lax.fori_loop(0, (near_count + BOND_UNROLL - 1) // BOND_UNROLL, step, 0)

    lane = iota((8, BLK), 1)
    rank = iota((8, BLK), 0)
    turn = (lane % 64) // 8 == rank
    half_lane = iota((1, BLK), 1)

    def far_step(n, carry):
        results = []
        for u in range(FAR_UNROLL):
            number = n * FAR_UNROLL + u
            good = number < far_count
            entry = far[jnp.where(good, number, 0)]
            g = entry // tile_count
            t = entry % tile_count
            a = tiles[2 * t, first + g]
            b = tiles[2 * t + 1, first + g]
            row_at = g * blocks + a
            col_at = g * blocks + b
            upper = jnp.where(b > a, 1, 0)
            own_words = bits[first + g, pl.ds(t, 1), pl.ds(pl.multiple_of(upper * 1024, 1024), 1024)]
            words = stack_rows(
                {r: own_words[:, r * BLK : r * BLK + BLK] for r in range(8)}, BLK, jnp.int32
            )
            flags = jnp.right_shift(words, lane // 16) & 1
            flags = jnp.where(lane % 16 == rank + 8 * (1 - upper), flags, 0).astype(F32)
            flags = jnp.concatenate([flags, jnp.zeros_like(flags)], axis=0).astype(BF16)
            flags = dot(flags, fold[...], 1, 0)[:8]
            broken = jnp.sum(jnp.where(turn, flags, 0.0), axis=0, keepdims=True)
            gap = pltpu.roll(spots[col_at], 64, 1) - spots[row_at]
            squares = gap * gap
            now_square = squares[0:1] + squares[1:2] + squares[2:3]
            bond = 1.0 / HORIZON - lax.rsqrt(now_square)
            kept = (half_lane // 64 == upper) & (broken < 0.5) & good
            bond = jnp.where(kept, BOND_STIFF * bond, 0.0)
            results.append((row_at, gap * bond))
        for row_at, gain in results:
            total[row_at] = total[row_at] + gain
        return carry

    lax.fori_loop(0, (far_count + FAR_UNROLL - 1) // FAR_UNROLL, far_step, 0)

    def finish(g, carry):
        for h in range(blocks):
            for c in range(3):
                force[pl.ds((c * blocks + h) * grains + g, 1), :] = total[g * blocks + h, c : c + 1, :]
        return carry

    lax.fori_loop(0, grains, finish, 0)


def contact_kernel(pairs, count, received, out, lefts, rights, sums, total):
    owners = received.shape[0]
    share = received.shape[1] // 6

    def prepare(n, carry):
        for u in range(OWNER_UNROLL * share):
            at = n * OWNER_UNROLL * share + u
            s = n * OWNER_UNROLL + u // share
            cc = u % share
            line = [received[s, cc * 6 + c : cc * 6 + c + 1, :] for c in range(6)]
            own = -0.5 * (line[0] * line[0] + line[1] * line[1] + line[2] * line[2])
            one = jnp.ones((1, BLK), F32)
            base = {0: line[0], 1: line[1], 2: line[2]}
            lefts[at] = left_rows(stack_rows({**base, 3: own, 4: one}, BLK))
            rights[at] = right_rows(stack_rows({**base, 3: one, 4: own}, BLK))
            first, second, _ = split3(stack_rows({0: line[3], 1: line[4], 2: line[5], 3: one}, BLK))
            both = jnp.concatenate([first, second], axis=0).astype(BF16)
            sums[at, :, :BLK] = both
            sums[at, :, BLK:] = both
            total[at] = jnp.zeros((8, BLK), F32)
        return carry

    lax.fori_loop(0, owners // OWNER_UNROLL, prepare, 0)
    live = count[0]

    def step(n, carry):
        results = []
        for u in range(PAIR_UNROLL):
            number = n * PAIR_UNROLL + u
            good = number < live
            at = jnp.where(good, number, 0)
            i = pairs[0, at]
            j = pairs[1, at]
            weight = jnp.exp2(dot(lefts[j], rights[i], 0, 0))
            high, low = split2(weight)
            gain_i = dot(sums[j], jnp.concatenate([high, low], axis=0), 1, 0)
            gain_j = dot(sums[i], jnp.concatenate([high, low], axis=1), 1, 1)
            results.append((i, jnp.where(good, gain_i[:8] + gain_i[8:], 0.0)))
            results.append((j, jnp.where(good, gain_j[:8] + gain_j[8:], 0.0)))
        for at, gain in results:
            total[at] = total[at] + gain
        return carry

    lax.fori_loop(0, (live + PAIR_UNROLL - 1) // PAIR_UNROLL, step, 0)

    def finish(s, carry):
        for cc in range(share):
            found = total[s * share + cc]
            weight = found[3:4]
            for c in range(3):
                out[s, cc * 3 + c : cc * 3 + c + 1, :] = (
                    received[s, cc * 6 + 3 + c : cc * 6 + 4 + c, :] * weight - found[c : c + 1]
                )
        return carry

    lax.fori_loop(0, owners, finish, 0)


def finish_kernel(cut, order, returned, place_a, bond_a, place_b, bond_b, velocity, force, speed, held):
    _, grains, count = velocity.shape
    owners = returned.shape[0]
    node_blocks = count // BLK
    share = returned.shape[1] // 3
    blocks = held.shape[0] // (3 * grains)

    def accept(d, carry):
        for cc in range(share):
            j = order[0, d * share + cc]
            row = (j % blocks) * grains + j // blocks
            for c in range(3):
                held[pl.ds(row + c * blocks * grains, 1), :] = returned[
                    d, cc * 3 + c : cc * 3 + c + 1, :
                ]
        return carry

    lax.fori_loop(0, owners, accept, 0)
    for group in range(grains // 8):
        rows = slice(group * 8, group * 8 + 8)
        for tile in range(count // BLK):
            span = slice(tile * BLK, tile * BLK + BLK)
            early = group * 8 < cut
            place, bond = (place_a, bond_a) if early else (place_b, bond_b)
            part = cut if early else grains - cut
            own = group * 8 - (0 if early else cut)
            base = tile * part + own
            code = place[base : base + 8, :]
            spot = code - 1
            low = spot & (BLK - 1)
            high = jnp.where(code == 0, -1, spot >> 7)
            for c in range(3):
                total = jnp.zeros((8, BLK), F32)
                for k in range(blocks):
                    at = (c * blocks + k) * grains + group * 8
                    found = jnp.take_along_axis(held[at : at + 8, :], low, axis=1)
                    total = jnp.where(high == k, found, total)
                near = (c * node_blocks + tile) * part + own
                total = bond[near : near + 8, :] + total
                force[c, rows, span] = total
                speed[c, rows, span] = velocity[c, rows, span] + TIME_STEP * total


def on_device(displacement, velocity, centers, tile_list, broken_bits, surface_nodes, send_order, pair_list, pair_count):
    grains, _, count = displacement.shape
    owners = lax.axis_size("grain") * lax.axis_size("cell")
    slots = send_order.shape[1]
    share = slots // owners
    surface = surface_nodes.shape[1]
    blocks = surface // BLK
    node_blocks = count // BLK
    tile_count = tile_list.shape[1]
    shift = displacement.transpose(1, 0, 2)
    speed = velocity.transpose(1, 0, 2)
    tiles = tile_list.transpose(1, 2, 0).reshape(2 * tile_count, grains)
    pairs = pair_list[0].T
    vmem = pl.BlockSpec(memory_space=pltpu.VMEM)
    smem = pl.BlockSpec(memory_space=pltpu.SMEM)
    hbm = pl.BlockSpec(memory_space=pltpu.HBM)
    params = pltpu.CompilerParams(vmem_limit_bytes=VMEM_BYTES)

    outgoing = pl.pallas_call(
        pick_kernel,
        out_shape=jax.ShapeDtypeStruct((owners, 6 * share, BLK), F32),
        in_specs=[smem, hbm, hbm, vmem, hbm],
        out_specs=vmem,
        scratch_shapes=[
            pltpu.VMEM((6 * slots, BLK), F32),
            pltpu.VMEM((3, grains, count), F32),
            pltpu.VMEM((3, grains, count), F32),
            pltpu.VMEM((grains, surface), jnp.int32),
            pltpu.SemaphoreType.DMA((3,)),
        ],
        compiler_params=pltpu.CompilerParams(vmem_limit_bytes=PICK_BYTES),
        name="pick",
    )(send_order, shift, speed, centers, surface_nodes)

    def bonds(first, part, shift_now):
        return pl.pallas_call(
            functools.partial(bond_kernel, first, part),
            out_shape=(
                jax.ShapeDtypeStruct((3 * node_blocks * part, BLK), F32),
                jax.ShapeDtypeStruct((node_blocks * part, BLK), jnp.int32),
            ),
            in_specs=[smem, vmem, vmem, vmem],
            out_specs=(vmem, vmem),
            scratch_shapes=[
                pltpu.VMEM((part * node_blocks, 48, BLK), BF16),
                pltpu.VMEM((part * node_blocks, 48, BLK), BF16),
                pltpu.VMEM((part * node_blocks, 32, 2 * BLK), BF16),
                pltpu.VMEM((part * node_blocks, 8, BLK), F32),
                pltpu.VMEM((part * node_blocks, 8, BLK), F32),
                pltpu.VMEM((3, BLK, BLK), F32),
                pltpu.VMEM((3, BLK, BLK), F32),
                pltpu.VMEM((3, BLK, BLK), jnp.int32),
                pltpu.VMEM((16, BLK), BF16),
                pltpu.VMEM((BLK, BLK), BF16),
                pltpu.SMEM((part * tile_count + 1,), jnp.int32),
                pltpu.SMEM((part * tile_count + 1,), jnp.int32),
            ],
            compiler_params=params,
            cost_estimate=pl.CostEstimate(
                flops=4_000_000_000, bytes_accessed=3_000_000, transcendentals=4_000_000
            ),
            name="bond",
        )(tiles, shift_now, broken_bits, surface_nodes)

    cut = grains * FIRST_SHARE // ALL_SHARES // 8 * 8
    outgoing, shift_now = lax.optimization_barrier((outgoing, shift))
    received = lax.all_to_all(outgoing, ("grain", "cell"), split_axis=0, concat_axis=0, tiled=True)
    bond_a, place_a = bonds(0, cut, shift_now)
    received, bond_a, place_a = lax.optimization_barrier((received, bond_a, place_a))

    slot_force = pl.pallas_call(
        contact_kernel,
        out_shape=jax.ShapeDtypeStruct((owners, 3 * share, BLK), F32),
        in_specs=[smem, smem, vmem],
        out_specs=vmem,
        scratch_shapes=[
            pltpu.VMEM((slots, 48, BLK), BF16),
            pltpu.VMEM((slots, 48, BLK), BF16),
            pltpu.VMEM((slots, 16, 2 * BLK), BF16),
            pltpu.VMEM((slots, 8, BLK), F32),
        ],
        compiler_params=params,
        name="contact",
    )(pairs, pair_count, received)

    slot_force, shift_now = lax.optimization_barrier((slot_force, shift_now))
    returned = lax.all_to_all(slot_force, ("grain", "cell"), split_axis=0, concat_axis=0, tiled=True)
    bond_b, place_b = bonds(cut, grains - cut, shift_now)

    force, new_speed = pl.pallas_call(
        functools.partial(finish_kernel, cut),
        out_shape=(jax.ShapeDtypeStruct((3, grains, count), F32),) * 2,
        in_specs=[smem, vmem, vmem, vmem, vmem, vmem, vmem],
        out_specs=(vmem, vmem),
        scratch_shapes=[pltpu.VMEM((3 * slots, BLK), F32)],
        compiler_params=params,
        name="finish",
    )(send_order, returned, place_a, bond_a, place_b, bond_b, speed)
    return force.transpose(1, 0, 2), new_speed.transpose(1, 0, 2)


def solution(mesh):
    own = ("grain", "cell")
    return jax.shard_map(
        on_device,
        mesh=mesh,
        in_specs=(
            P(own, None, None),
            P(own, None, None),
            P(None, own),
            P(own, None, None),
            P(own, None, None),
            P(own, None),
            P(own, None),
            P(own, None, None),
            P(own),
        ),
        out_specs=(P(own, None, None), P(own, None, None)),
        check_vma=False,
    )
```

```python
import functools
import math

import jax
import jax.numpy as jnp
from jax import lax
from jax.experimental import pallas as pl
from jax.experimental.pallas import tpu as pltpu
from jax.sharding import PartitionSpec as P

BLK = 128
HORIZON = 3.0
BOND_STIFF = 5.0
CONTACT_STIFF = 0.02
CONTACT_DAMP = 0.05
CONTACT_RANGE = 9.0
TIME_STEP = 0.5
VMEM_BYTES = 32 * 1024 * 1024
PICK_BYTES = 60 * 1024 * 1024
FAR = 100.0
BOND_UNROLL = 8
FAR_UNROLL = 4
PAIR_UNROLL = 16
GRAIN_UNROLL = 4
OWNER_UNROLL = 2
FIRST_SHARE = 6
ALL_SHARES = 8
F32 = jnp.float32
BF16 = jnp.bfloat16


def iota(shape, axis):
    return lax.broadcasted_iota(jnp.int32, shape, axis)


def split3(value):
    one = value.astype(BF16).astype(F32)
    rest = value - one
    two = rest.astype(BF16).astype(F32)
    return one, two, (rest - two).astype(BF16).astype(F32)


def left_rows(value):
    one, two, three = split3(value)
    return jnp.concatenate([one, one, two, one, three, two], axis=0).astype(BF16)


def right_rows(value):
    one, two, three = split3(value)
    return jnp.concatenate([one, two, one, three, one, two], axis=0).astype(BF16)


def dot(left, right, left_dim, right_dim):
    return lax.dot_general(
        left, right, (((left_dim,), (right_dim,)), ((), ())), preferred_element_type=F32
    )


def split2(value):
    high = value.astype(BF16)
    return high, (value - high.astype(F32)).astype(BF16)


def stack_rows(pieces, width, kind=F32):
    row = iota((8, width), 0)
    total = jnp.zeros((8, width), kind)
    for number, piece in pieces.items():
        total = jnp.where(row == number, jnp.broadcast_to(piece, (8, width)), total)
    return total


def lattice_row(node):
    return (
        (node % 8).astype(F32) - 3.5,
        (node // 8 % 8).astype(F32) - 3.5,
        (node // 64).astype(F32) - 5.5,
    )


def pick_kernel(order, shift_in, velocity_in, centers, nodes_in, out, held, shift, velocity, nodes, arrived):
    copies = [
        pltpu.make_async_copy(source, target, arrived.at[number])
        for number, (source, target) in enumerate(
            ((shift_in, shift), (velocity_in, velocity), (nodes_in, nodes))
        )
    ]
    for copy in copies:
        copy.start()
    _, grains, count = shift.shape
    surface = nodes.shape[1]
    blocks = surface // BLK
    owners = out.shape[0]
    share = out.shape[1] // 6
    scale = math.sqrt(2.0 * math.log2(math.e) / CONTACT_RANGE)
    same = iota((grains, grains), 0) == iota((grains, grains), 1)
    offsets = [
        jnp.sum(jnp.where(same, centers[c : c + 1, :], 0.0), axis=1, keepdims=True)
        for c in range(3)
    ]
    for copy in copies:
        copy.wait()
    for group in range(grains // 8):
        rows = slice(group * 8, group * 8 + 8)
        places = []
        speeds = []
        for tile in range(count // BLK):
            span = slice(tile * BLK, tile * BLK + BLK)
            rest = lattice_row(iota((8, BLK), 1) + tile * BLK)
            now = [rest[c] + shift[c, rows, span] + offsets[c][rows] for c in range(3)]
            places.append([scale * now[c] for c in range(3)])
            speeds.append(
                [
                    CONTACT_STIFF * now[c] - CONTACT_DAMP * velocity[c, rows, span]
                    for c in range(3)
                ]
            )
        for k in range(blocks):
            index = nodes[rows, k * BLK : k * BLK + BLK]
            low = index & (BLK - 1)
            high = index >> 7
            for c in range(6):
                source = places if c < 3 else speeds
                total = jnp.zeros((8, BLK), F32)
                for tile in range(count // BLK):
                    found = jnp.take_along_axis(source[tile][c % 3], low, axis=1)
                    total = jnp.where(high == tile, found, total)
                base = (c * blocks + k) * grains + group * 8
                held[base : base + 8, :] = total

    def send(d, carry):
        for cc in range(share):
            j = order[0, d * share + cc]
            row = (j % blocks) * grains + j // blocks
            for c in range(6):
                out[d, cc * 6 + c : cc * 6 + c + 1, :] = held[
                    pl.ds(row + c * blocks * grains, 1), :
                ]
        return carry

    lax.fori_loop(0, owners, send, 0)


def bond_kernel(first, grains, tiles, shift, bits, nodes, *refs):
    handed = (len(refs) - 15) // 2
    for listing, listing_out in zip(refs[:handed], refs[handed + 2 :]):
        listing_out[...] = listing[...]
    force, place = refs[handed : handed + 2]
    lefts, rights, sums, spots, total, inverse, square, dead, spread, fold, fixed, near, far = refs[-13:]
    count = shift.shape[2]
    tile_count = bits.shape[1]
    surface = nodes.shape[1]
    blocks = count // BLK

    q = iota((BLK, BLK), 0)
    p = iota((BLK, BLK), 1)
    flat = (q % 8 - p % 8) ** 2 + (q // 8 % 8 - p // 8 % 8) ** 2
    for delta in range(-1, 2):
        squared = (flat + (2 * delta + q // 64 - p // 64) ** 2).astype(F32)
        kept = (squared > 0.25) & (squared <= HORIZON * HORIZON)
        square[delta + 1] = jnp.where(kept, squared, FAR)
        inverse[delta + 1] = 1.0 / jnp.sqrt(jnp.where(kept, squared, FAR))
        dead[delta + 1] = jnp.where(kept, 0, 255)
    fold[...] = jnp.where(q // 16 == p % 8, 1.0, 0.0).astype(BF16)
    spread[...] = jnp.where(iota((16, BLK), 1) % 16 == iota((16, BLK), 0), 1.0, 0.0).astype(BF16)

    wide = (8, count)
    row = iota(wide, 0)
    rest = lattice_row(iota(wide, 1))
    rest_rows = jnp.where(row == 0, rest[0], jnp.where(row == 1, rest[1], jnp.where(row == 2, rest[2], 0.0)))
    fixed[0] = rest_rows
    fixed[1] = pltpu.roll(rest_rows, 3, 0) + jnp.where(row == 7, 1.0, 0.0)
    fixed[2] = rest_rows - jnp.where(row == 6, 0.5, 0.0)
    fixed[3] = rest_rows + jnp.where(row == 3, 1.0, 0.0)
    ids = iota((BLK, BLK), 0).astype(F32).astype(BF16)

    def prepare_one(g):
        moved = stack_rows({c: shift[c, pl.ds(first + g, 1), :] for c in range(3)}, count)
        own = jnp.sum(moved * (moved + 2.0 * fixed[0]), axis=0, keepdims=True)
        left = jnp.where(row == 6, own, moved + fixed[1])
        right = jnp.where(row == 7, own, -2.0 * (moved + pltpu.roll(moved, 3, 0) + fixed[2]))
        spot = moved + fixed[3]
        left_all = left_rows(left)
        right_all = right_rows(right)
        one, two, three = split3(spot)
        sum_all = jnp.concatenate([one, two, three, jnp.zeros_like(one)], axis=0).astype(BF16)

        listed = nodes[pl.ds(first + g, 1), :]
        low = (listed & (BLK - 1)).astype(F32).astype(BF16)
        high = listed >> 7
        position = iota((1, surface), 1)
        hit = iota((8, surface), 0) == jnp.broadcast_to(high, (8, surface))
        within = jnp.where(hit, jnp.broadcast_to((position % BLK + 1).astype(F32), (8, surface)), 0.0)
        group = jnp.where(hit, jnp.broadcast_to((position // BLK).astype(F32), (8, surface)), 0.0)
        chosen = jnp.concatenate([within, group], axis=0).astype(BF16)
        match = jnp.concatenate(
            [
                jnp.where(
                    ids == jnp.broadcast_to(low[:, k * BLK : k * BLK + BLK], (BLK, BLK)),
                    jnp.ones((BLK, BLK), BF16),
                    jnp.zeros((BLK, BLK), BF16),
                )
                for k in range(surface // BLK)
            ],
            axis=1,
        )
        found = dot(chosen, match, 1, 1)
        code = (found[:8] + float(BLK) * found[8:]).astype(jnp.int32)
        return left_all, right_all, sum_all, spot, code

    def prepare(n, carry):
        ready = [(n * GRAIN_UNROLL + u, prepare_one(n * GRAIN_UNROLL + u)) for u in range(GRAIN_UNROLL)]
        for g, (left_all, right_all, sum_all, spot, code) in ready:
            for h in range(blocks):
                span = slice(h * BLK, h * BLK + BLK)
                at = g * blocks + h
                lefts[at] = left_all[:, span]
                rights[at] = right_all[:, span]
                sums[at, :, :BLK] = sum_all[:, span]
                sums[at, :, BLK:] = sum_all[:, span]
                spots[at] = spot[:, span]
                total[at] = jnp.zeros((8, BLK), F32)
                place[pl.ds(h * grains + g, 1), :] = code[h : h + 1, :]
        return carry

    lax.fori_loop(0, grains // GRAIN_UNROLL, prepare, 0)

    def enlist(g, carry):
        near_held, far_held = carry
        for t in range(tile_count):
            gap = tiles[2 * t + 1, first + g] - tiles[2 * t, first + g]
            near[near_held] = g * tile_count + t
            far[far_held] = g * tile_count + t
            near_held = near_held + jnp.where((gap <= 1) & (gap >= -1), 1, 0)
            far_held = far_held + jnp.where((gap == 2) | (gap == -2), 1, 0)
        return near_held, far_held

    near_count, far_count = lax.fori_loop(0, grains, enlist, (0, 0))
    own_group = (iota((8, BLK), 1) // 16) == iota((8, BLK), 0)
    flag_all = jnp.left_shift(1, iota((BLK, BLK), 0) % 8)

    def step(n, carry):
        results = []
        for u in range(BOND_UNROLL):
            number = n * BOND_UNROLL + u
            good = number < near_count
            entry = near[jnp.where(good, number, 0)]
            g = entry // tile_count
            t = entry % tile_count
            a = tiles[2 * t, first + g]
            b = tiles[2 * t + 1, first + g]
            row_at = g * blocks + a
            col_at = g * blocks + b
            delta = b - a + 1
            excess = dot(lefts[col_at], rights[row_at], 0, 0)
            words = bits[first + g, pl.ds(t, 1), :].astype(F32)
            sorted_words = jnp.concatenate(
                [
                    jnp.where(
                        own_group,
                        jnp.broadcast_to(words[:, w * BLK : w * BLK + BLK], (8, BLK)),
                        0.0,
                    )
                    for w in range(16)
                ],
                axis=0,
            ).astype(BF16)
            turned = dot(spread[...], sorted_words, 1, 1).astype(jnp.int32)
            bond = inverse[delta] - lax.rsqrt(square[delta] + excess)
            flags = jnp.concatenate(
                [jnp.broadcast_to(turned[w : w + 1], (8, BLK)) for w in range(16)], axis=0
            )
            bond = jnp.where(((flags | dead[delta]) & flag_all) == 0, bond, 0.0)
            high, low = split2(bond)
            found = dot(sums[col_at], jnp.concatenate([high, low], axis=0), 1, 0)
            found = found[:8] + found[8:16] + found[16:24]
            gain = BOND_STIFF * (found - spots[row_at] * found[3:4])
            results.append((row_at, jnp.where(good, gain, 0.0)))
        for row_at, gain in results:
            total[row_at] = total[row_at] + gain
        return carry

    lax.fori_loop(0, (near_count + BOND_UNROLL - 1) // BOND_UNROLL, step, 0)

    lane = iota((8, BLK), 1)
    rank = iota((8, BLK), 0)
    turn = (lane % 64) // 8 == rank
    half_lane = iota((1, BLK), 1)

    def far_step(n, carry):
        results = []
        for u in range(FAR_UNROLL):
            number = n * FAR_UNROLL + u
            good = number < far_count
            entry = far[jnp.where(good, number, 0)]
            g = entry // tile_count
            t = entry % tile_count
            a = tiles[2 * t, first + g]
            b = tiles[2 * t + 1, first + g]
            row_at = g * blocks + a
            col_at = g * blocks + b
            upper = jnp.where(b > a, 1, 0)
            own_words = bits[first + g, pl.ds(t, 1), pl.ds(pl.multiple_of(upper * 1024, 1024), 1024)]
            words = stack_rows(
                {r: own_words[:, r * BLK : r * BLK + BLK] for r in range(8)}, BLK, jnp.int32
            )
            flags = jnp.right_shift(words, lane // 16) & 1
            flags = jnp.where(lane % 16 == rank + 8 * (1 - upper), flags, 0).astype(F32)
            flags = jnp.concatenate([flags, jnp.zeros_like(flags)], axis=0).astype(BF16)
            flags = dot(flags, fold[...], 1, 0)[:8]
            broken = jnp.sum(jnp.where(turn, flags, 0.0), axis=0, keepdims=True)
            gap = pltpu.roll(spots[col_at], 64, 1) - spots[row_at]
            squares = gap * gap
            now_square = squares[0:1] + squares[1:2] + squares[2:3]
            bond = 1.0 / HORIZON - lax.rsqrt(now_square)
            kept = (half_lane // 64 == upper) & (broken < 0.5) & good
            bond = jnp.where(kept, BOND_STIFF * bond, 0.0)
            results.append((row_at, gap * bond))
        for row_at, gain in results:
            total[row_at] = total[row_at] + gain
        return carry

    lax.fori_loop(0, (far_count + FAR_UNROLL - 1) // FAR_UNROLL, far_step, 0)

    def finish(g, carry):
        for h in range(blocks):
            for c in range(3):
                force[pl.ds((c * blocks + h) * grains + g, 1), :] = total[g * blocks + h, c : c + 1, :]
        return carry

    lax.fori_loop(0, grains, finish, 0)


def contact_kernel(pairs, count, received, out, lefts, rights, sums, total):
    owners = received.shape[0]
    share = received.shape[1] // 6
    row = iota((8, BLK), 0)
    third = jnp.where(row == 3, 1.0, 0.0)
    fourth = jnp.where(row == 4, 1.0, 0.0)

    def prepare(n, carry):
        for u in range(OWNER_UNROLL * share):
            at = n * OWNER_UNROLL * share + u
            s = n * OWNER_UNROLL + u // share
            cc = u % share
            line = received[s, cc * 6 : cc * 6 + 6, :]
            line = jnp.concatenate([line, jnp.zeros((2, BLK), F32)], axis=0)
            place = jnp.where(row < 3, line, 0.0)
            own = -0.5 * jnp.sum(place * place, axis=0, keepdims=True)
            lefts[at] = left_rows(jnp.where(row == 3, own, place + fourth))
            rights[at] = right_rows(jnp.where(row == 4, own, place + third))
            high, low, _ = split3(jnp.where(row == 6, 1.0, jnp.where(row < 3, 0.0, line)))
            both = jnp.concatenate([high, low], axis=0).astype(BF16)
            sums[at, :, :BLK] = both
            sums[at, :, BLK:] = both
            total[at] = jnp.zeros((8, BLK), F32)
        return carry

    lax.fori_loop(0, owners // OWNER_UNROLL, prepare, 0)
    live = count[0]

    def step(n, carry):
        results = []
        for u in range(PAIR_UNROLL):
            number = n * PAIR_UNROLL + u
            good = number < live
            at = jnp.where(good, number, 0)
            i = pairs[0, at]
            j = pairs[1, at]
            weight = jnp.exp2(dot(lefts[j], rights[i], 0, 0))
            high, low = split2(weight)
            gain_i = dot(sums[j], jnp.concatenate([high, low], axis=0), 1, 0)
            gain_j = dot(sums[i], jnp.concatenate([high, low], axis=1), 1, 1)
            results.append((i, jnp.where(good, gain_i[:8] + gain_i[8:], 0.0)))
            results.append((j, jnp.where(good, gain_j[:8] + gain_j[8:], 0.0)))
        for at, gain in results:
            total[at] = total[at] + gain
        return carry

    lax.fori_loop(0, (live + PAIR_UNROLL - 1) // PAIR_UNROLL, step, 0)

    def finish(s, carry):
        for cc in range(share):
            found = total[s * share + cc]
            speeds = received[s, cc * 6 + 3 : cc * 6 + 6, :]
            out[s, cc * 3 : cc * 3 + 3, :] = speeds * found[6:7] - found[3:6]
        return carry

    lax.fori_loop(0, owners, finish, 0)


def finish_kernel(cut, order, returned, place_a, bond_a, place_b, bond_b, velocity, force, speed, held):
    _, grains, count = velocity.shape
    owners = returned.shape[0]
    node_blocks = count // BLK
    share = returned.shape[1] // 3
    blocks = held.shape[0] // (3 * grains)

    def accept(d, carry):
        for cc in range(share):
            j = order[0, d * share + cc]
            row = (j % blocks) * grains + j // blocks
            for c in range(3):
                held[pl.ds(row + c * blocks * grains, 1), :] = returned[
                    d, cc * 3 + c : cc * 3 + c + 1, :
                ]
        return carry

    lax.fori_loop(0, owners, accept, 0)
    for group in range(grains // 8):
        rows = slice(group * 8, group * 8 + 8)
        for tile in range(count // BLK):
            span = slice(tile * BLK, tile * BLK + BLK)
            early = group * 8 < cut
            place, bond = (place_a, bond_a) if early else (place_b, bond_b)
            part = cut if early else grains - cut
            own = group * 8 - (0 if early else cut)
            base = tile * part + own
            code = place[base : base + 8, :]
            spot = code - 1
            low = spot & (BLK - 1)
            high = jnp.where(code == 0, -1, spot >> 7)
            for c in range(3):
                total = jnp.zeros((8, BLK), F32)
                for k in range(blocks):
                    at = (c * blocks + k) * grains + group * 8
                    found = jnp.take_along_axis(held[at : at + 8, :], low, axis=1)
                    total = jnp.where(high == k, found, total)
                near = (c * node_blocks + tile) * part + own
                total = bond[near : near + 8, :] + total
                force[c, rows, span] = total
                speed[c, rows, span] = velocity[c, rows, span] + TIME_STEP * total


def on_device(displacement, velocity, centers, tile_list, broken_bits, surface_nodes, send_order, pair_list, pair_count):
    grains, _, count = displacement.shape
    owners = lax.axis_size("grain") * lax.axis_size("cell")
    slots = send_order.shape[1]
    share = slots // owners
    surface = surface_nodes.shape[1]
    blocks = surface // BLK
    node_blocks = count // BLK
    tile_count = tile_list.shape[1]
    shift = displacement.transpose(1, 0, 2)
    speed = velocity.transpose(1, 0, 2)
    tiles = tile_list.transpose(1, 2, 0).reshape(2 * tile_count, grains)
    pairs = pair_list[0].T
    vmem = pl.BlockSpec(memory_space=pltpu.VMEM)
    smem = pl.BlockSpec(memory_space=pltpu.SMEM)
    hbm = pl.BlockSpec(memory_space=pltpu.HBM)
    params = pltpu.CompilerParams(vmem_limit_bytes=VMEM_BYTES)

    outgoing = pl.pallas_call(
        pick_kernel,
        out_shape=jax.ShapeDtypeStruct((owners, 6 * share, BLK), F32),
        in_specs=[smem, hbm, hbm, vmem, hbm],
        out_specs=vmem,
        scratch_shapes=[
            pltpu.VMEM((6 * slots, BLK), F32),
            pltpu.VMEM((3, grains, count), F32),
            pltpu.VMEM((3, grains, count), F32),
            pltpu.VMEM((grains, surface), jnp.int32),
            pltpu.SemaphoreType.DMA((3,)),
        ],
        compiler_params=pltpu.CompilerParams(vmem_limit_bytes=PICK_BYTES),
        name="pick",
    )(send_order, shift, speed, centers, surface_nodes)

    def bonds(first, part, shift_now, *listings):
        return pl.pallas_call(
            functools.partial(bond_kernel, first, part),
            out_shape=(
                jax.ShapeDtypeStruct((3 * node_blocks * part, BLK), F32),
                jax.ShapeDtypeStruct((node_blocks * part, BLK), jnp.int32),
                *[jax.ShapeDtypeStruct(listing.shape, jnp.int32) for listing in listings],
            ),
            in_specs=[smem, vmem, vmem, vmem] + [vmem] * len(listings),
            out_specs=(vmem,) * (2 + len(listings)),
            scratch_shapes=[
                pltpu.VMEM((part * node_blocks, 48, BLK), BF16),
                pltpu.VMEM((part * node_blocks, 48, BLK), BF16),
                pltpu.VMEM((part * node_blocks, 32, 2 * BLK), BF16),
                pltpu.VMEM((part * node_blocks, 8, BLK), F32),
                pltpu.VMEM((part * node_blocks, 8, BLK), F32),
                pltpu.VMEM((3, BLK, BLK), F32),
                pltpu.VMEM((3, BLK, BLK), F32),
                pltpu.VMEM((3, BLK, BLK), jnp.int32),
                pltpu.VMEM((16, BLK), BF16),
                pltpu.VMEM((BLK, BLK), BF16),
                pltpu.VMEM((4, 8, count), F32),
                pltpu.SMEM((part * tile_count + 1,), jnp.int32),
                pltpu.SMEM((part * tile_count + 1,), jnp.int32),
            ],
            compiler_params=params,
            cost_estimate=pl.CostEstimate(
                flops=4_000_000_000, bytes_accessed=3_000_000, transcendentals=4_000_000
            ),
            name="bond",
        )(tiles, shift_now, broken_bits, surface_nodes, *listings)

    cut = grains * FIRST_SHARE // ALL_SHARES // 8 * 8
    outgoing, shift_now = lax.optimization_barrier((outgoing, shift))
    received = lax.all_to_all(outgoing, ("grain", "cell"), split_axis=0, concat_axis=0, tiled=True)
    bond_a, place_a, pairs, order = bonds(0, cut, shift_now, pairs, send_order)
    received, bond_a, place_a = lax.optimization_barrier((received, bond_a, place_a))

    slot_force = pl.pallas_call(
        contact_kernel,
        out_shape=jax.ShapeDtypeStruct((owners, 3 * share, BLK), F32),
        in_specs=[smem, smem, vmem],
        out_specs=vmem,
        scratch_shapes=[
            pltpu.VMEM((slots, 48, BLK), BF16),
            pltpu.VMEM((slots, 48, BLK), BF16),
            pltpu.VMEM((slots, 16, 2 * BLK), BF16),
            pltpu.VMEM((slots, 8, BLK), F32),
        ],
        compiler_params=params,
        name="contact",
    )(pairs, pair_count, received)

    slot_force, shift_now = lax.optimization_barrier((slot_force, shift_now))
    returned = lax.all_to_all(slot_force, ("grain", "cell"), split_axis=0, concat_axis=0, tiled=True)
    bond_b, place_b = bonds(cut, grains - cut, shift_now)

    force, new_speed = pl.pallas_call(
        functools.partial(finish_kernel, cut),
        out_shape=(jax.ShapeDtypeStruct((3, grains, count), F32),) * 2,
        in_specs=[smem, vmem, vmem, vmem, vmem, vmem, vmem],
        out_specs=(vmem, vmem),
        scratch_shapes=[pltpu.VMEM((3 * slots, BLK), F32)],
        compiler_params=params,
        name="finish",
    )(order, returned, place_a, bond_a, place_b, bond_b, speed)
    return force.transpose(1, 0, 2), new_speed.transpose(1, 0, 2)


def solution(mesh):
    own = ("grain", "cell")
    return jax.shard_map(
        on_device,
        mesh=mesh,
        in_specs=(
            P(own, None, None),
            P(own, None, None),
            P(None, own),
            P(own, None, None),
            P(own, None, None),
            P(own, None),
            P(own, None),
            P(own, None, None),
            P(own),
        ),
        out_specs=(P(own, None, None), P(own, None, None)),
        check_vma=False,
    )
```

```python
import functools
import math

import jax
import jax.numpy as jnp
from jax import lax
from jax.experimental import pallas as pl
from jax.experimental.pallas import tpu as pltpu
from jax.sharding import PartitionSpec as P

BLK = 128
HORIZON = 3.0
BOND_STIFF = 5.0
CONTACT_STIFF = 0.02
CONTACT_DAMP = 0.05
CONTACT_RANGE = 9.0
TIME_STEP = 0.5
VMEM_BYTES = 32 * 1024 * 1024
PICK_BYTES = 60 * 1024 * 1024
FAR = 100.0
BOND_UNROLL = 8
FAR_UNROLL = 4
PAIR_UNROLL = 16
GRAIN_UNROLL = 4
OWNER_UNROLL = 2
FIRST_SHARE = 5
ALL_SHARES = 8
F32 = jnp.float32
BF16 = jnp.bfloat16


def iota(shape, axis):
    return lax.broadcasted_iota(jnp.int32, shape, axis)


def split3(value):
    one = value.astype(BF16).astype(F32)
    rest = value - one
    two = rest.astype(BF16).astype(F32)
    return one, two, (rest - two).astype(BF16).astype(F32)


def left_rows(value):
    one, two, three = split3(value)
    return jnp.concatenate([one, one, two, one, three, two], axis=0).astype(BF16)


def right_rows(value):
    one, two, three = split3(value)
    return jnp.concatenate([one, two, one, three, one, two], axis=0).astype(BF16)


def dot(left, right, left_dim, right_dim):
    return lax.dot_general(
        left, right, (((left_dim,), (right_dim,)), ((), ())), preferred_element_type=F32
    )


def split2(value):
    high = value.astype(BF16)
    return high, (value - high.astype(F32)).astype(BF16)


def stack_rows(pieces, width, kind=F32):
    row = iota((8, width), 0)
    total = jnp.zeros((8, width), kind)
    for number, piece in pieces.items():
        total = jnp.where(row == number, jnp.broadcast_to(piece, (8, width)), total)
    return total


def lattice_row(node):
    return (
        (node % 8).astype(F32) - 3.5,
        (node // 8 % 8).astype(F32) - 3.5,
        (node // 64).astype(F32) - 5.5,
    )


def pick_kernel(order, shift_in, velocity_in, centers, nodes_in, out, held, shift, velocity, nodes, arrived):
    copies = [
        pltpu.make_async_copy(source, target, arrived.at[number])
        for number, (source, target) in enumerate(
            ((shift_in, shift), (velocity_in, velocity), (nodes_in, nodes))
        )
    ]
    for copy in copies:
        copy.start()
    _, grains, count = shift.shape
    surface = nodes.shape[1]
    blocks = surface // BLK
    owners = out.shape[0]
    share = out.shape[1] // 6
    scale = math.sqrt(2.0 * math.log2(math.e) / CONTACT_RANGE)
    same = iota((grains, grains), 0) == iota((grains, grains), 1)
    offsets = [
        jnp.sum(jnp.where(same, centers[c : c + 1, :], 0.0), axis=1, keepdims=True)
        for c in range(3)
    ]
    for copy in copies:
        copy.wait()
    for group in range(grains // 8):
        rows = slice(group * 8, group * 8 + 8)
        places = []
        speeds = []
        for tile in range(count // BLK):
            span = slice(tile * BLK, tile * BLK + BLK)
            rest = lattice_row(iota((8, BLK), 1) + tile * BLK)
            now = [rest[c] + shift[c, rows, span] + offsets[c][rows] for c in range(3)]
            places.append([scale * now[c] for c in range(3)])
            speeds.append(
                [
                    CONTACT_STIFF * now[c] - CONTACT_DAMP * velocity[c, rows, span]
                    for c in range(3)
                ]
            )
        for k in range(blocks):
            index = nodes[rows, k * BLK : k * BLK + BLK]
            low = index & (BLK - 1)
            high = index >> 7
            for c in range(6):
                source = places if c < 3 else speeds
                total = jnp.zeros((8, BLK), F32)
                for tile in range(count // BLK):
                    found = jnp.take_along_axis(source[tile][c % 3], low, axis=1)
                    total = jnp.where(high == tile, found, total)
                base = (c * blocks + k) * grains + group * 8
                held[base : base + 8, :] = total

    def send(d, carry):
        for cc in range(share):
            j = order[0, d * share + cc]
            row = (j % blocks) * grains + j // blocks
            for c in range(6):
                out[d, cc * 6 + c : cc * 6 + c + 1, :] = held[
                    pl.ds(row + c * blocks * grains, 1), :
                ]
        return carry

    lax.fori_loop(0, owners, send, 0)


def bond_kernel(first, grains, tiles, shift, bits, nodes, *refs):
    handed = (len(refs) - 15) // 2
    for listing, listing_out in zip(refs[:handed], refs[handed + 2 :]):
        listing_out[...] = listing[...]
    force, place = refs[handed : handed + 2]
    lefts, rights, sums, spots, total, inverse, square, dead, spread, fold, fixed, near, far = refs[-13:]
    count = shift.shape[2]
    tile_count = bits.shape[1]
    surface = nodes.shape[1]
    blocks = count // BLK

    q = iota((BLK, BLK), 0)
    p = iota((BLK, BLK), 1)
    flat = (q % 8 - p % 8) ** 2 + (q // 8 % 8 - p // 8 % 8) ** 2
    for delta in range(-1, 2):
        squared = (flat + (2 * delta + q // 64 - p // 64) ** 2).astype(F32)
        kept = (squared > 0.25) & (squared <= HORIZON * HORIZON)
        square[delta + 1] = jnp.where(kept, squared, FAR)
        inverse[delta + 1] = 1.0 / jnp.sqrt(jnp.where(kept, squared, FAR))
        dead[delta + 1] = jnp.where(kept, 0, 255)
    fold[...] = jnp.where(q // 16 == p % 8, 1.0, 0.0).astype(BF16)
    spread[...] = jnp.where(iota((16, BLK), 1) % 16 == iota((16, BLK), 0), 1.0, 0.0).astype(BF16)

    wide = (8, count)
    row = iota(wide, 0)
    rest = lattice_row(iota(wide, 1))
    rest_rows = jnp.where(row == 0, rest[0], jnp.where(row == 1, rest[1], jnp.where(row == 2, rest[2], 0.0)))
    fixed[0] = rest_rows
    fixed[1] = pltpu.roll(rest_rows, 3, 0) + jnp.where(row == 7, 1.0, 0.0)
    fixed[2] = rest_rows - jnp.where(row == 6, 0.5, 0.0)
    fixed[3] = rest_rows + jnp.where(row == 3, 1.0, 0.0)
    ids = iota((BLK, BLK), 0).astype(F32).astype(BF16)

    def prepare_one(g):
        moved = stack_rows({c: shift[c, pl.ds(first + g, 1), :] for c in range(3)}, count)
        own = jnp.sum(moved * (moved + 2.0 * fixed[0]), axis=0, keepdims=True)
        left = jnp.where(row == 6, own, moved + fixed[1])
        right = jnp.where(row == 7, own, -2.0 * (moved + pltpu.roll(moved, 3, 0) + fixed[2]))
        spot = moved + fixed[3]
        left_all = left_rows(left)
        right_all = right_rows(right)
        one, two, three = split3(spot)
        sum_all = jnp.concatenate([one, two, three, jnp.zeros_like(one)], axis=0).astype(BF16)

        listed = nodes[pl.ds(first + g, 1), :]
        low = (listed & (BLK - 1)).astype(F32).astype(BF16)
        high = listed >> 7
        position = iota((1, surface), 1)
        hit = iota((8, surface), 0) == jnp.broadcast_to(high, (8, surface))
        within = jnp.where(hit, jnp.broadcast_to((position % BLK + 1).astype(F32), (8, surface)), 0.0)
        group = jnp.where(hit, jnp.broadcast_to((position // BLK).astype(F32), (8, surface)), 0.0)
        chosen = jnp.concatenate([within, group], axis=0).astype(BF16)
        match = jnp.concatenate(
            [
                jnp.where(
                    ids == jnp.broadcast_to(low[:, k * BLK : k * BLK + BLK], (BLK, BLK)),
                    jnp.ones((BLK, BLK), BF16),
                    jnp.zeros((BLK, BLK), BF16),
                )
                for k in range(surface // BLK)
            ],
            axis=1,
        )
        found = dot(chosen, match, 1, 1)
        code = (found[:8] + float(BLK) * found[8:]).astype(jnp.int32)
        return left_all, right_all, sum_all, spot, code

    def prepare(n, carry):
        ready = [(n * GRAIN_UNROLL + u, prepare_one(n * GRAIN_UNROLL + u)) for u in range(GRAIN_UNROLL)]
        for g, (left_all, right_all, sum_all, spot, code) in ready:
            for h in range(blocks):
                span = slice(h * BLK, h * BLK + BLK)
                at = g * blocks + h
                lefts[at] = left_all[:, span]
                rights[at] = right_all[:, span]
                sums[at, :, :BLK] = sum_all[:, span]
                sums[at, :, BLK:] = sum_all[:, span]
                spots[at] = spot[:, span]
                total[at] = jnp.zeros((8, BLK), F32)
                place[pl.ds(h * grains + g, 1), :] = code[h : h + 1, :]
        return carry

    lax.fori_loop(0, grains // GRAIN_UNROLL, prepare, 0)

    def enlist(g, carry):
        near_held, far_held = carry
        for t in range(tile_count):
            gap = tiles[2 * t + 1, first + g] - tiles[2 * t, first + g]
            near[near_held] = g * tile_count + t
            far[far_held] = g * tile_count + t
            near_held = near_held + jnp.where((gap <= 1) & (gap >= -1), 1, 0)
            far_held = far_held + jnp.where((gap == 2) | (gap == -2), 1, 0)
        return near_held, far_held

    near_count, far_count = lax.fori_loop(0, grains, enlist, (0, 0))
    own_group = (iota((8, BLK), 1) // 16) == iota((8, BLK), 0)
    flag_all = jnp.left_shift(1, iota((BLK, BLK), 0) % 8)

    def step(n, carry):
        entries = []
        for u in range(BOND_UNROLL):
            number = n * BOND_UNROLL + u
            good = number < near_count
            entry = near[jnp.where(good, number, 0)]
            g = entry // tile_count
            t = entry % tile_count
            a = tiles[2 * t, first + g]
            b = tiles[2 * t + 1, first + g]
            entries.append((good, g, t, g * blocks + a, g * blocks + b, b - a + 1))
        sorted_words = []
        for _, g, t, *_ in entries:
            words = bits[first + g, pl.ds(t, 1), :].astype(F32)
            for w in range(16):
                spread_row = jnp.broadcast_to(words[:, w * BLK : w * BLK + BLK], (8, BLK))
                sorted_words.append(jnp.where(own_group, spread_row, 0.0))
        sorted_words = jnp.concatenate(sorted_words, axis=0).astype(BF16)
        turned = dot(spread[...], sorted_words, 1, 1).astype(jnp.int32)
        halves = []
        for u, (_, _, _, row_at, col_at, delta) in enumerate(entries):
            excess = dot(lefts[col_at], rights[row_at], 0, 0)
            bond = inverse[delta] - lax.rsqrt(square[delta] + excess)
            own_flags = turned[:, u * BLK : u * BLK + BLK]
            flags = jnp.concatenate(
                [jnp.broadcast_to(own_flags[w : w + 1], (8, BLK)) for w in range(16)], axis=0
            )
            bond = jnp.where(((flags | dead[delta]) & flag_all) == 0, bond, 0.0)
            halves.append(jnp.concatenate(split2(bond), axis=0))
        results = []
        for u in range(0, BOND_UNROLL, 2):
            left = jnp.concatenate([sums[entries[v][4]] for v in (u, u + 1)], axis=0)
            both = dot(left, jnp.concatenate(halves[u : u + 2], axis=1), 1, 0)
            for v in range(2):
                good, _, _, row_at, _, _ = entries[u + v]
                found = both[v * 32 : v * 32 + 32, v * BLK : v * BLK + BLK]
                found = found[:8] + found[8:16] + found[16:24]
                gain = BOND_STIFF * (found - spots[row_at] * found[3:4])
                results.append((row_at, jnp.where(good, gain, 0.0)))
        for row_at, gain in results:
            total[row_at] = total[row_at] + gain
        return carry

    lax.fori_loop(0, (near_count + BOND_UNROLL - 1) // BOND_UNROLL, step, 0)

    lane = iota((8, BLK), 1)
    rank = iota((8, BLK), 0)
    turn = (lane % 64) // 8 == rank
    half_lane = iota((1, BLK), 1)

    def far_step(n, carry):
        results = []
        for u in range(FAR_UNROLL):
            number = n * FAR_UNROLL + u
            good = number < far_count
            entry = far[jnp.where(good, number, 0)]
            g = entry // tile_count
            t = entry % tile_count
            a = tiles[2 * t, first + g]
            b = tiles[2 * t + 1, first + g]
            row_at = g * blocks + a
            col_at = g * blocks + b
            upper = jnp.where(b > a, 1, 0)
            own_words = bits[first + g, pl.ds(t, 1), pl.ds(pl.multiple_of(upper * 1024, 1024), 1024)]
            words = stack_rows(
                {r: own_words[:, r * BLK : r * BLK + BLK] for r in range(8)}, BLK, jnp.int32
            )
            flags = jnp.right_shift(words, lane // 16) & 1
            flags = jnp.where(lane % 16 == rank + 8 * (1 - upper), flags, 0).astype(F32)
            flags = jnp.concatenate([flags, jnp.zeros_like(flags)], axis=0).astype(BF16)
            flags = dot(flags, fold[...], 1, 0)[:8]
            broken = jnp.sum(jnp.where(turn, flags, 0.0), axis=0, keepdims=True)
            gap = pltpu.roll(spots[col_at], 64, 1) - spots[row_at]
            squares = gap * gap
            now_square = squares[0:1] + squares[1:2] + squares[2:3]
            bond = 1.0 / HORIZON - lax.rsqrt(now_square)
            kept = (half_lane // 64 == upper) & (broken < 0.5) & good
            bond = jnp.where(kept, BOND_STIFF * bond, 0.0)
            results.append((row_at, gap * bond))
        for row_at, gain in results:
            total[row_at] = total[row_at] + gain
        return carry

    lax.fori_loop(0, (far_count + FAR_UNROLL - 1) // FAR_UNROLL, far_step, 0)

    def finish(g, carry):
        for h in range(blocks):
            for c in range(3):
                force[pl.ds((c * blocks + h) * grains + g, 1), :] = total[g * blocks + h, c : c + 1, :]
        return carry

    lax.fori_loop(0, grains, finish, 0)


def contact_kernel(pairs, count, received, out, lefts, rights, sums, total):
    owners = received.shape[0]
    share = received.shape[1] // 6
    row = iota((8, BLK), 0)
    third = jnp.where(row == 3, 1.0, 0.0)
    fourth = jnp.where(row == 4, 1.0, 0.0)

    def prepare(n, carry):
        for u in range(OWNER_UNROLL * share):
            at = n * OWNER_UNROLL * share + u
            s = n * OWNER_UNROLL + u // share
            cc = u % share
            line = received[s, cc * 6 : cc * 6 + 6, :]
            line = jnp.concatenate([line, jnp.zeros((2, BLK), F32)], axis=0)
            place = jnp.where(row < 3, line, 0.0)
            own = -0.5 * jnp.sum(place * place, axis=0, keepdims=True)
            lefts[at] = left_rows(jnp.where(row == 3, own, place + fourth))
            rights[at] = right_rows(jnp.where(row == 4, own, place + third))
            high, low, _ = split3(jnp.where(row == 6, 1.0, jnp.where(row < 3, 0.0, line)))
            both = jnp.concatenate([high, low], axis=0).astype(BF16)
            sums[at, :, :BLK] = both
            sums[at, :, BLK:] = both
            total[at] = jnp.zeros((8, BLK), F32)
        return carry

    lax.fori_loop(0, owners // OWNER_UNROLL, prepare, 0)
    live = count[0]

    def step(n, carry):
        ready = []
        for u in range(PAIR_UNROLL):
            number = n * PAIR_UNROLL + u
            good = number < live
            at = jnp.where(good, number, 0)
            i = pairs[0, at]
            j = pairs[1, at]
            high, low = split2(jnp.exp2(dot(lefts[j], rights[i], 0, 0)))
            ready.append((i, j, good, high, low))
        results = []
        for u in range(0, PAIR_UNROLL, 2):
            two = ready[u : u + 2]
            upright = jnp.concatenate(
                [jnp.concatenate([high, low], axis=0) for *_, high, low in two], axis=1
            )
            flat = jnp.concatenate(
                [jnp.concatenate([high, low], axis=1) for *_, high, low in two], axis=0
            )
            gain_i = dot(jnp.concatenate([sums[j] for _, j, *_ in two], axis=0), upright, 1, 0)
            gain_j = dot(jnp.concatenate([sums[i] for i, *_ in two], axis=0), flat, 1, 1)
            for v, (i, j, good, _, _) in enumerate(two):
                span = slice(v * BLK, v * BLK + BLK)
                for at, gain in ((i, gain_i), (j, gain_j)):
                    gain = gain[v * 16 : v * 16 + 8, span] + gain[v * 16 + 8 : v * 16 + 16, span]
                    results.append((at, jnp.where(good, gain, 0.0)))
        for at, gain in results:
            total[at] = total[at] + gain
        return carry

    lax.fori_loop(0, (live + PAIR_UNROLL - 1) // PAIR_UNROLL, step, 0)

    def finish(s, carry):
        for cc in range(share):
            found = total[s * share + cc]
            speeds = received[s, cc * 6 + 3 : cc * 6 + 6, :]
            out[s, cc * 3 : cc * 3 + 3, :] = speeds * found[6:7] - found[3:6]
        return carry

    lax.fori_loop(0, owners, finish, 0)


def finish_kernel(cut, order, returned, place_a, bond_a, place_b, bond_b, velocity, force, speed, held):
    _, grains, count = velocity.shape
    owners = returned.shape[0]
    node_blocks = count // BLK
    share = returned.shape[1] // 3
    blocks = held.shape[0] // (3 * grains)

    def accept(d, carry):
        for cc in range(share):
            j = order[0, d * share + cc]
            row = (j % blocks) * grains + j // blocks
            for c in range(3):
                held[pl.ds(row + c * blocks * grains, 1), :] = returned[
                    d, cc * 3 + c : cc * 3 + c + 1, :
                ]
        return carry

    lax.fori_loop(0, owners, accept, 0)

    def rows_of(early, late, group, part):
        start, end = group * 8, group * 8 + 8
        pieces = []
        if start < cut:
            pieces.append(early[part * cut + start : part * cut + min(end, cut), :])
        if end > cut:
            base = part * (grains - cut) - cut
            pieces.append(late[base + max(start, cut) : base + end, :])
        return pieces[0] if len(pieces) == 1 else jnp.concatenate(pieces, axis=0)

    for group in range(grains // 8):
        rows = slice(group * 8, group * 8 + 8)
        for tile in range(count // BLK):
            span = slice(tile * BLK, tile * BLK + BLK)
            code = rows_of(place_a, place_b, group, tile)
            spot = code - 1
            low = spot & (BLK - 1)
            high = jnp.where(code == 0, -1, spot >> 7)
            for c in range(3):
                total = jnp.zeros((8, BLK), F32)
                for k in range(blocks):
                    at = (c * blocks + k) * grains + group * 8
                    found = jnp.take_along_axis(held[at : at + 8, :], low, axis=1)
                    total = jnp.where(high == k, found, total)
                total = rows_of(bond_a, bond_b, group, c * node_blocks + tile) + total
                force[c, rows, span] = total
                speed[c, rows, span] = velocity[c, rows, span] + TIME_STEP * total


def on_device(displacement, velocity, centers, tile_list, broken_bits, surface_nodes, send_order, pair_list, pair_count):
    grains, _, count = displacement.shape
    owners = lax.axis_size("grain") * lax.axis_size("cell")
    slots = send_order.shape[1]
    share = slots // owners
    surface = surface_nodes.shape[1]
    blocks = surface // BLK
    node_blocks = count // BLK
    tile_count = tile_list.shape[1]
    shift = displacement.transpose(1, 0, 2)
    speed = velocity.transpose(1, 0, 2)
    tiles = tile_list.transpose(1, 2, 0).reshape(2 * tile_count, grains)
    pairs = pair_list[0].T
    vmem = pl.BlockSpec(memory_space=pltpu.VMEM)
    smem = pl.BlockSpec(memory_space=pltpu.SMEM)
    hbm = pl.BlockSpec(memory_space=pltpu.HBM)
    params = pltpu.CompilerParams(vmem_limit_bytes=VMEM_BYTES)

    outgoing = pl.pallas_call(
        pick_kernel,
        out_shape=jax.ShapeDtypeStruct((owners, 6 * share, BLK), F32),
        in_specs=[smem, hbm, hbm, vmem, hbm],
        out_specs=vmem,
        scratch_shapes=[
            pltpu.VMEM((6 * slots, BLK), F32),
            pltpu.VMEM((3, grains, count), F32),
            pltpu.VMEM((3, grains, count), F32),
            pltpu.VMEM((grains, surface), jnp.int32),
            pltpu.SemaphoreType.DMA((3,)),
        ],
        compiler_params=pltpu.CompilerParams(vmem_limit_bytes=PICK_BYTES),
        name="pick",
    )(send_order, shift, speed, centers, surface_nodes)

    def bonds(first, part, shift_now, *listings):
        return pl.pallas_call(
            functools.partial(bond_kernel, first, part),
            out_shape=(
                jax.ShapeDtypeStruct((3 * node_blocks * part, BLK), F32),
                jax.ShapeDtypeStruct((node_blocks * part, BLK), jnp.int32),
                *[jax.ShapeDtypeStruct(listing.shape, jnp.int32) for listing in listings],
            ),
            in_specs=[smem, vmem, vmem, vmem] + [vmem] * len(listings),
            out_specs=(vmem,) * (2 + len(listings)),
            scratch_shapes=[
                pltpu.VMEM((part * node_blocks, 48, BLK), BF16),
                pltpu.VMEM((part * node_blocks, 48, BLK), BF16),
                pltpu.VMEM((part * node_blocks, 32, 2 * BLK), BF16),
                pltpu.VMEM((part * node_blocks, 8, BLK), F32),
                pltpu.VMEM((part * node_blocks, 8, BLK), F32),
                pltpu.VMEM((3, BLK, BLK), F32),
                pltpu.VMEM((3, BLK, BLK), F32),
                pltpu.VMEM((3, BLK, BLK), jnp.int32),
                pltpu.VMEM((16, BLK), BF16),
                pltpu.VMEM((BLK, BLK), BF16),
                pltpu.VMEM((4, 8, count), F32),
                pltpu.SMEM((part * tile_count + 1,), jnp.int32),
                pltpu.SMEM((part * tile_count + 1,), jnp.int32),
            ],
            compiler_params=params,
            cost_estimate=pl.CostEstimate(
                flops=4_000_000_000, bytes_accessed=3_000_000, transcendentals=4_000_000
            ),
            name="bond",
        )(tiles, shift_now, broken_bits, surface_nodes, *listings)

    cut = grains * FIRST_SHARE // ALL_SHARES // GRAIN_UNROLL * GRAIN_UNROLL
    outgoing, shift_now = lax.optimization_barrier((outgoing, shift))
    received = lax.all_to_all(outgoing, ("grain", "cell"), split_axis=0, concat_axis=0, tiled=True)
    bond_a, place_a, pairs, order = bonds(0, cut, shift_now, pairs, send_order)
    received, bond_a, place_a = lax.optimization_barrier((received, bond_a, place_a))

    slot_force = pl.pallas_call(
        contact_kernel,
        out_shape=jax.ShapeDtypeStruct((owners, 3 * share, BLK), F32),
        in_specs=[smem, smem, vmem],
        out_specs=vmem,
        scratch_shapes=[
            pltpu.VMEM((slots, 48, BLK), BF16),
            pltpu.VMEM((slots, 48, BLK), BF16),
            pltpu.VMEM((slots, 16, 2 * BLK), BF16),
            pltpu.VMEM((slots, 8, BLK), F32),
        ],
        compiler_params=params,
        name="contact",
    )(pairs, pair_count, received)

    slot_force, shift_now = lax.optimization_barrier((slot_force, shift_now))
    returned = lax.all_to_all(slot_force, ("grain", "cell"), split_axis=0, concat_axis=0, tiled=True)
    bond_b, place_b = bonds(cut, grains - cut, shift_now)

    force, new_speed = pl.pallas_call(
        functools.partial(finish_kernel, cut),
        out_shape=(jax.ShapeDtypeStruct((3, grains, count), F32),) * 2,
        in_specs=[smem, vmem, vmem, vmem, vmem, vmem, vmem],
        out_specs=(vmem, vmem),
        scratch_shapes=[pltpu.VMEM((3 * slots, BLK), F32)],
        compiler_params=params,
        name="finish",
    )(order, returned, place_a, bond_a, place_b, bond_b, speed)
    return force.transpose(1, 0, 2), new_speed.transpose(1, 0, 2)


def solution(mesh):
    own = ("grain", "cell")
    return jax.shard_map(
        on_device,
        mesh=mesh,
        in_specs=(
            P(own, None, None),
            P(own, None, None),
            P(None, own),
            P(own, None, None),
            P(own, None, None),
            P(own, None),
            P(own, None),
            P(own, None, None),
            P(own),
        ),
        out_specs=(P(own, None, None), P(own, None, None)),
        check_vma=False,
    )
```

```python
import functools
import math

import jax
import jax.numpy as jnp
from jax import lax
from jax.experimental import pallas as pl
from jax.experimental.pallas import tpu as pltpu
from jax.sharding import PartitionSpec as P

BLK = 128
HORIZON = 3.0
BOND_STIFF = 5.0
CONTACT_STIFF = 0.02
CONTACT_DAMP = 0.05
CONTACT_RANGE = 9.0
TIME_STEP = 0.5
VMEM_BYTES = 32 * 1024 * 1024
PICK_BYTES = 60 * 1024 * 1024
FAR = 100.0
BOND_UNROLL = 8
FAR_UNROLL = 4
PAIR_UNROLL = 16
GRAIN_UNROLL = 4
ROW_UNROLL = 2
OWNER_UNROLL = 4
FIRST_SHARE = 5
ALL_SHARES = 8
F32 = jnp.float32
BF16 = jnp.bfloat16


def iota(shape, axis):
    return lax.broadcasted_iota(jnp.int32, shape, axis)


def split3(value):
    one = value.astype(BF16).astype(F32)
    rest = value - one
    two = rest.astype(BF16).astype(F32)
    return one, two, (rest - two).astype(BF16).astype(F32)


def left_rows(value):
    one, two, three = split3(value)
    return jnp.concatenate([one, one, two, one, three, two], axis=0).astype(BF16)


def right_rows(value):
    one, two, three = split3(value)
    return jnp.concatenate([one, two, one, three, one, two], axis=0).astype(BF16)


def dot(left, right, left_dim, right_dim):
    return lax.dot_general(
        left, right, (((left_dim,), (right_dim,)), ((), ())), preferred_element_type=F32
    )


def split2(value):
    high = value.astype(BF16)
    return high, (value - high.astype(F32)).astype(BF16)


def stack_rows(pieces, width, kind=F32):
    row = iota((8, width), 0)
    total = jnp.zeros((8, width), kind)
    for number, piece in pieces.items():
        total = jnp.where(row == number, jnp.broadcast_to(piece, (8, width)), total)
    return total


def lattice_row(node):
    return (
        (node % 8).astype(F32) - 3.5,
        (node // 8 % 8).astype(F32) - 3.5,
        (node // 64).astype(F32) - 5.5,
    )


def pick_kernel(order, shift_in, velocity_in, centers, nodes_in, out, held, shift, velocity, nodes, arrived):
    copies = [
        pltpu.make_async_copy(source, target, arrived.at[number])
        for number, (source, target) in enumerate(
            ((shift_in, shift), (velocity_in, velocity), (nodes_in, nodes))
        )
    ]
    for copy in copies:
        copy.start()
    _, grains, count = shift.shape
    surface = nodes.shape[1]
    blocks = surface // BLK
    owners = out.shape[0]
    share = out.shape[1] // 6
    scale = math.sqrt(2.0 * math.log2(math.e) / CONTACT_RANGE)
    same = iota((grains, grains), 0) == iota((grains, grains), 1)
    offsets = [
        jnp.sum(jnp.where(same, centers[c : c + 1, :], 0.0), axis=1, keepdims=True)
        for c in range(3)
    ]
    for copy in copies:
        copy.wait()
    for group in range(grains // 8):
        rows = slice(group * 8, group * 8 + 8)
        places = []
        speeds = []
        for tile in range(count // BLK):
            span = slice(tile * BLK, tile * BLK + BLK)
            rest = lattice_row(iota((8, BLK), 1) + tile * BLK)
            now = [rest[c] + shift[c, rows, span] + offsets[c][rows] for c in range(3)]
            places.append([scale * now[c] for c in range(3)])
            speeds.append(
                [
                    CONTACT_STIFF * now[c] - CONTACT_DAMP * velocity[c, rows, span]
                    for c in range(3)
                ]
            )
        index = [nodes[rows, k * BLK : k * BLK + BLK] for k in range(blocks)]
        low = [one & (BLK - 1) for one in index]
        high = [one >> 7 for one in index]
        found = [[jnp.zeros((8, BLK), F32)] * 6 for _ in range(blocks)]
        for tile in range(count // BLK):
            sources = places[tile] + speeds[tile]
            for k in range(blocks):
                here = high[k] == tile
                found[k] = [
                    jnp.where(here, jnp.take_along_axis(sources[c], low[k], axis=1), found[k][c])
                    for c in range(6)
                ]
        for k in range(blocks):
            for c in range(6):
                base = (c * blocks + k) * grains + group * 8
                held[base : base + 8, :] = found[k][c]

    def send(n, carry):
        moved = []
        for u in range(ROW_UNROLL):
            d = n * ROW_UNROLL + u
            for cc in range(share):
                j = order[0, d * share + cc]
                row = (j % blocks) * grains + j // blocks
                for c in range(6):
                    moved.append((d, cc * 6 + c, held[pl.ds(row + c * blocks * grains, 1), :]))
        for d, at, line in moved:
            out[d, at : at + 1, :] = line
        return carry

    lax.fori_loop(0, owners // ROW_UNROLL, send, 0)


def bond_kernel(first, grains, tiles, shift, bits, nodes, *refs):
    handed = (len(refs) - 15) // 2
    for listing, listing_out in zip(refs[:handed], refs[handed + 2 :]):
        listing_out[...] = listing[...]
    force, place = refs[handed : handed + 2]
    lefts, rights, sums, spots, total, inverse, square, dead, spread, fold, fixed, near, far = refs[-13:]
    count = shift.shape[2]
    tile_count = bits.shape[1]
    surface = nodes.shape[1]
    blocks = count // BLK

    q = iota((BLK, BLK), 0)
    p = iota((BLK, BLK), 1)
    flat = (q % 8 - p % 8) ** 2 + (q // 8 % 8 - p // 8 % 8) ** 2
    for delta in range(-1, 2):
        squared = (flat + (2 * delta + q // 64 - p // 64) ** 2).astype(F32)
        kept = (squared > 0.25) & (squared <= HORIZON * HORIZON)
        square[delta + 1] = jnp.where(kept, squared, FAR)
        inverse[delta + 1] = 1.0 / jnp.sqrt(jnp.where(kept, squared, FAR))
        dead[delta + 1] = jnp.where(kept, 0, 255)
    fold[...] = jnp.where(q // 16 == p % 8, 1.0, 0.0).astype(BF16)
    spread[...] = jnp.where(iota((16, BLK), 1) % 16 == iota((16, BLK), 0), 1.0, 0.0).astype(BF16)

    wide = (8, count)
    row = iota(wide, 0)
    rest = lattice_row(iota(wide, 1))
    rest_rows = jnp.where(row == 0, rest[0], jnp.where(row == 1, rest[1], jnp.where(row == 2, rest[2], 0.0)))
    fixed[0] = rest_rows
    fixed[1] = pltpu.roll(rest_rows, 3, 0) + jnp.where(row == 7, 1.0, 0.0)
    fixed[2] = rest_rows - jnp.where(row == 6, 0.5, 0.0)
    fixed[3] = rest_rows + jnp.where(row == 3, 1.0, 0.0)
    ids = iota((BLK, BLK), 0).astype(F32).astype(BF16)

    def prepare_one(g):
        moved = stack_rows({c: shift[c, pl.ds(first + g, 1), :] for c in range(3)}, count)
        own = jnp.sum(moved * (moved + 2.0 * fixed[0]), axis=0, keepdims=True)
        left = jnp.where(row == 6, own, moved + fixed[1])
        right = jnp.where(row == 7, own, -2.0 * (moved + pltpu.roll(moved, 3, 0) + fixed[2]))
        spot = moved + fixed[3]
        left_all = left_rows(left)
        right_all = right_rows(right)
        one, two, three = split3(spot)
        sum_all = jnp.concatenate([one, two, three, jnp.zeros_like(one)], axis=0).astype(BF16)

        listed = nodes[pl.ds(first + g, 1), :]
        low = (listed & (BLK - 1)).astype(F32).astype(BF16)
        high = listed >> 7
        position = iota((1, surface), 1)
        hit = iota((8, surface), 0) == jnp.broadcast_to(high, (8, surface))
        within = jnp.where(hit, jnp.broadcast_to((position % BLK + 1).astype(F32), (8, surface)), 0.0)
        group = jnp.where(hit, jnp.broadcast_to((position // BLK).astype(F32), (8, surface)), 0.0)
        chosen = jnp.concatenate([within, group], axis=0).astype(BF16)
        match = jnp.concatenate(
            [
                jnp.where(
                    ids == jnp.broadcast_to(low[:, k * BLK : k * BLK + BLK], (BLK, BLK)),
                    jnp.ones((BLK, BLK), BF16),
                    jnp.zeros((BLK, BLK), BF16),
                )
                for k in range(surface // BLK)
            ],
            axis=1,
        )
        found = dot(chosen, match, 1, 1)
        code = (found[:8] + float(BLK) * found[8:]).astype(jnp.int32)
        return left_all, right_all, sum_all, spot, code

    def prepare(n, carry):
        ready = [(n * GRAIN_UNROLL + u, prepare_one(n * GRAIN_UNROLL + u)) for u in range(GRAIN_UNROLL)]
        for g, (left_all, right_all, sum_all, spot, code) in ready:
            for h in range(blocks):
                span = slice(h * BLK, h * BLK + BLK)
                at = g * blocks + h
                lefts[at] = left_all[:, span]
                rights[at] = right_all[:, span]
                sums[at, :, :BLK] = sum_all[:, span]
                sums[at, :, BLK:] = sum_all[:, span]
                spots[at] = spot[:, span]
                total[at] = jnp.zeros((8, BLK), F32)
                place[pl.ds(h * grains + g, 1), :] = code[h : h + 1, :]
        return carry

    lax.fori_loop(0, grains // GRAIN_UNROLL, prepare, 0)

    def enlist(g, carry):
        near_held, far_held = carry
        for t in range(tile_count):
            gap = tiles[2 * t + 1, first + g] - tiles[2 * t, first + g]
            near[near_held] = g * tile_count + t
            far[far_held] = g * tile_count + t
            near_held = near_held + jnp.where((gap <= 1) & (gap >= -1), 1, 0)
            far_held = far_held + jnp.where((gap == 2) | (gap == -2), 1, 0)
        return near_held, far_held

    near_count, far_count = lax.fori_loop(0, grains, enlist, (0, 0))
    own_group = (iota((8, BLK), 1) // 16) == iota((8, BLK), 0)
    flag_all = jnp.left_shift(1, iota((BLK, BLK), 0) % 8)

    def step(n, carry):
        entries = []
        for u in range(BOND_UNROLL):
            number = n * BOND_UNROLL + u
            good = number < near_count
            entry = near[jnp.where(good, number, 0)]
            g = entry // tile_count
            t = entry % tile_count
            a = tiles[2 * t, first + g]
            b = tiles[2 * t + 1, first + g]
            entries.append((good, g, t, g * blocks + a, g * blocks + b, b - a + 1))
        sorted_words = []
        for _, g, t, *_ in entries:
            words = bits[first + g, pl.ds(t, 1), :].astype(F32)
            for w in range(16):
                spread_row = jnp.broadcast_to(words[:, w * BLK : w * BLK + BLK], (8, BLK))
                sorted_words.append(jnp.where(own_group, spread_row, 0.0))
        sorted_words = jnp.concatenate(sorted_words, axis=0).astype(BF16)
        turned = dot(spread[...], sorted_words, 1, 1).astype(jnp.int32)
        halves = []
        for u, (_, _, _, row_at, col_at, delta) in enumerate(entries):
            excess = dot(lefts[col_at], rights[row_at], 0, 0)
            bond = inverse[delta] - lax.rsqrt(square[delta] + excess)
            own_flags = turned[:, u * BLK : u * BLK + BLK]
            flags = jnp.concatenate(
                [jnp.broadcast_to(own_flags[w : w + 1], (8, BLK)) for w in range(16)], axis=0
            )
            bond = jnp.where(((flags | dead[delta]) & flag_all) == 0, bond, 0.0)
            halves.append(jnp.concatenate(split2(bond), axis=0))
        results = []
        for u in range(0, BOND_UNROLL, 2):
            left = jnp.concatenate([sums[entries[v][4]] for v in (u, u + 1)], axis=0)
            both = dot(left, jnp.concatenate(halves[u : u + 2], axis=1), 1, 0)
            for v in range(2):
                good, _, _, row_at, _, _ = entries[u + v]
                found = both[v * 32 : v * 32 + 32, v * BLK : v * BLK + BLK]
                found = found[:8] + found[8:16] + found[16:24]
                gain = BOND_STIFF * (found - spots[row_at] * found[3:4])
                results.append((row_at, jnp.where(good, gain, 0.0)))
        for row_at, gain in results:
            total[row_at] = total[row_at] + gain
        return carry

    lax.fori_loop(0, (near_count + BOND_UNROLL - 1) // BOND_UNROLL, step, 0)

    lane = iota((8, BLK), 1)
    rank = iota((8, BLK), 0)
    turn = (lane % 64) // 8 == rank
    half_lane = iota((1, BLK), 1)

    def far_step(n, carry):
        results = []
        for u in range(FAR_UNROLL):
            number = n * FAR_UNROLL + u
            good = number < far_count
            entry = far[jnp.where(good, number, 0)]
            g = entry // tile_count
            t = entry % tile_count
            a = tiles[2 * t, first + g]
            b = tiles[2 * t + 1, first + g]
            row_at = g * blocks + a
            col_at = g * blocks + b
            upper = jnp.where(b > a, 1, 0)
            own_words = bits[first + g, pl.ds(t, 1), pl.ds(pl.multiple_of(upper * 1024, 1024), 1024)]
            words = stack_rows(
                {r: own_words[:, r * BLK : r * BLK + BLK] for r in range(8)}, BLK, jnp.int32
            )
            flags = jnp.right_shift(words, lane // 16) & 1
            flags = jnp.where(lane % 16 == rank + 8 * (1 - upper), flags, 0).astype(F32)
            flags = jnp.concatenate([flags, jnp.zeros_like(flags)], axis=0).astype(BF16)
            flags = dot(flags, fold[...], 1, 0)[:8]
            broken = jnp.sum(jnp.where(turn, flags, 0.0), axis=0, keepdims=True)
            gap = pltpu.roll(spots[col_at], 64, 1) - spots[row_at]
            squares = gap * gap
            now_square = squares[0:1] + squares[1:2] + squares[2:3]
            bond = 1.0 / HORIZON - lax.rsqrt(now_square)
            kept = (half_lane // 64 == upper) & (broken < 0.5) & good
            bond = jnp.where(kept, BOND_STIFF * bond, 0.0)
            results.append((row_at, gap * bond))
        for row_at, gain in results:
            total[row_at] = total[row_at] + gain
        return carry

    lax.fori_loop(0, (far_count + FAR_UNROLL - 1) // FAR_UNROLL, far_step, 0)

    def finish(g, carry):
        for h in range(blocks):
            for c in range(3):
                force[pl.ds((c * blocks + h) * grains + g, 1), :] = total[g * blocks + h, c : c + 1, :]
        return carry

    lax.fori_loop(0, grains, finish, 0)


def contact_kernel(pairs, count, received, out, lefts, rights, sums, total):
    owners = received.shape[0]
    share = received.shape[1] // 6
    row = iota((8, BLK), 0)
    third = jnp.where(row == 3, 1.0, 0.0)
    fourth = jnp.where(row == 4, 1.0, 0.0)

    def prepare(n, carry):
        slots = range(OWNER_UNROLL * share)
        base = n * OWNER_UNROLL * share
        blank = jnp.zeros((2, BLK), F32)
        lines = []
        for u in slots:
            line = received[n * OWNER_UNROLL + u // share, u % share * 6 : u % share * 6 + 6, :]
            lines.append(jnp.concatenate([line, blank], axis=0))
        spots = [jnp.where(row < 3, line, 0.0) for line in lines]
        owns = [-0.5 * jnp.sum(spot * spot, axis=0, keepdims=True) for spot in spots]
        left = [left_rows(jnp.where(row == 3, own, spot + fourth)) for spot, own in zip(spots, owns)]
        right = [right_rows(jnp.where(row == 4, own, spot + third)) for spot, own in zip(spots, owns)]
        both = []
        for line in lines:
            high, low = split2(jnp.where(row == 6, 1.0, jnp.where(row < 3, 0.0, line)))
            both.append(jnp.concatenate([high.astype(F32), low.astype(F32)], axis=0).astype(BF16))
        for u in slots:
            at = base + u
            lefts[at] = left[u]
            rights[at] = right[u]
            sums[at, :, :BLK] = both[u]
            sums[at, :, BLK:] = both[u]
            total[at] = jnp.zeros((8, BLK), F32)
        return carry

    lax.fori_loop(0, owners // OWNER_UNROLL, prepare, 0)
    live = count[0]

    def step(n, carry):
        ready = []
        for u in range(PAIR_UNROLL):
            number = n * PAIR_UNROLL + u
            good = number < live
            at = jnp.where(good, number, 0)
            i = pairs[0, at]
            j = pairs[1, at]
            high, low = split2(jnp.exp2(dot(lefts[j], rights[i], 0, 0)))
            ready.append((i, j, good, high, low))
        results = []
        for u in range(0, PAIR_UNROLL, 2):
            two = ready[u : u + 2]
            upright = jnp.concatenate(
                [jnp.concatenate([high, low], axis=0) for *_, high, low in two], axis=1
            )
            flat = jnp.concatenate(
                [jnp.concatenate([high, low], axis=1) for *_, high, low in two], axis=0
            )
            gain_i = dot(jnp.concatenate([sums[j] for _, j, *_ in two], axis=0), upright, 1, 0)
            gain_j = dot(jnp.concatenate([sums[i] for i, *_ in two], axis=0), flat, 1, 1)
            for v, (i, j, good, _, _) in enumerate(two):
                span = slice(v * BLK, v * BLK + BLK)
                for at, gain in ((i, gain_i), (j, gain_j)):
                    gain = gain[v * 16 : v * 16 + 8, span] + gain[v * 16 + 8 : v * 16 + 16, span]
                    results.append((at, jnp.where(good, gain, 0.0)))
        for at, gain in results:
            total[at] = total[at] + gain
        return carry

    lax.fori_loop(0, (live + PAIR_UNROLL - 1) // PAIR_UNROLL, step, 0)

    def finish(n, carry):
        results = []
        for u in range(ROW_UNROLL):
            s = n * ROW_UNROLL + u
            for cc in range(share):
                found = total[s * share + cc]
                speeds = received[s, cc * 6 + 3 : cc * 6 + 6, :]
                results.append((s, cc, speeds * found[6:7] - found[3:6]))
        for s, cc, force in results:
            for c in range(3):
                out[s, c, cc : cc + 1, :] = force[c : c + 1]
        return carry

    lax.fori_loop(0, owners // ROW_UNROLL, finish, 0)


def finish_kernel(cut, order, returned, place_a, bond_a, place_b, bond_b, velocity, force, speed, held):
    _, grains, count = velocity.shape
    owners = returned.shape[0]
    node_blocks = count // BLK
    share = returned.shape[2]
    blocks = held.shape[0] // (3 * grains)

    def accept(n, carry):
        moved = []
        for u in range(ROW_UNROLL):
            d = n * ROW_UNROLL + u
            for cc in range(share):
                j = order[0, d * share + cc]
                row = (j % blocks) * grains + j // blocks
                for c in range(3):
                    moved.append((row + c * blocks * grains, returned[d, c, cc : cc + 1, :]))
        for at, line in moved:
            held[pl.ds(at, 1), :] = line
        return carry

    lax.fori_loop(0, owners // ROW_UNROLL, accept, 0)

    def rows_of(early, late, group, part):
        start, end = group * 8, group * 8 + 8
        pieces = []
        if start < cut:
            pieces.append(early[part * cut + start : part * cut + min(end, cut), :])
        if end > cut:
            base = part * (grains - cut) - cut
            pieces.append(late[base + max(start, cut) : base + end, :])
        return pieces[0] if len(pieces) == 1 else jnp.concatenate(pieces, axis=0)

    for group in range(grains // 8):
        rows = slice(group * 8, group * 8 + 8)
        codes = [rows_of(place_a, place_b, group, tile) for tile in range(node_blocks)]
        low = [(code - 1) & (BLK - 1) for code in codes]
        high = [jnp.where(code == 0, -1, (code - 1) >> 7) for code in codes]
        found = [[jnp.zeros((8, BLK), F32)] * 3 for _ in codes]
        for k in range(blocks):
            sources = [
                held[(c * blocks + k) * grains + group * 8 : (c * blocks + k) * grains + group * 8 + 8, :]
                for c in range(3)
            ]
            for tile in range(node_blocks):
                here = high[tile] == k
                found[tile] = [
                    jnp.where(here, jnp.take_along_axis(sources[c], low[tile], axis=1), found[tile][c])
                    for c in range(3)
                ]
        for tile in range(node_blocks):
            span = slice(tile * BLK, tile * BLK + BLK)
            for c in range(3):
                total = rows_of(bond_a, bond_b, group, c * node_blocks + tile) + found[tile][c]
                force[c, rows, span] = total
                speed[c, rows, span] = velocity[c, rows, span] + TIME_STEP * total


def on_device(displacement, velocity, centers, tile_list, broken_bits, surface_nodes, send_order, pair_list, pair_count):
    grains, _, count = displacement.shape
    owners = lax.axis_size("grain") * lax.axis_size("cell")
    slots = send_order.shape[1]
    share = slots // owners
    surface = surface_nodes.shape[1]
    blocks = surface // BLK
    node_blocks = count // BLK
    tile_count = tile_list.shape[1]
    shift = displacement.transpose(1, 0, 2)
    speed = velocity.transpose(1, 0, 2)
    tiles = tile_list.transpose(1, 2, 0).reshape(2 * tile_count, grains)
    pairs = pair_list[0].T
    vmem = pl.BlockSpec(memory_space=pltpu.VMEM)
    smem = pl.BlockSpec(memory_space=pltpu.SMEM)
    hbm = pl.BlockSpec(memory_space=pltpu.HBM)
    params = pltpu.CompilerParams(vmem_limit_bytes=VMEM_BYTES)

    outgoing = pl.pallas_call(
        pick_kernel,
        out_shape=jax.ShapeDtypeStruct((owners, 6 * share, BLK), F32),
        in_specs=[smem, hbm, hbm, vmem, hbm],
        out_specs=vmem,
        scratch_shapes=[
            pltpu.VMEM((6 * slots, BLK), F32),
            pltpu.VMEM((3, grains, count), F32),
            pltpu.VMEM((3, grains, count), F32),
            pltpu.VMEM((grains, surface), jnp.int32),
            pltpu.SemaphoreType.DMA((3,)),
        ],
        compiler_params=pltpu.CompilerParams(vmem_limit_bytes=PICK_BYTES),
        name="pick",
    )(send_order, shift, speed, centers, surface_nodes)

    def bonds(first, part, shift_now, *listings):
        return pl.pallas_call(
            functools.partial(bond_kernel, first, part),
            out_shape=(
                jax.ShapeDtypeStruct((3 * node_blocks * part, BLK), F32),
                jax.ShapeDtypeStruct((node_blocks * part, BLK), jnp.int32),
                *[jax.ShapeDtypeStruct(listing.shape, jnp.int32) for listing in listings],
            ),
            in_specs=[smem, vmem, vmem, vmem] + [vmem] * len(listings),
            out_specs=(vmem,) * (2 + len(listings)),
            scratch_shapes=[
                pltpu.VMEM((part * node_blocks, 48, BLK), BF16),
                pltpu.VMEM((part * node_blocks, 48, BLK), BF16),
                pltpu.VMEM((part * node_blocks, 32, 2 * BLK), BF16),
                pltpu.VMEM((part * node_blocks, 8, BLK), F32),
                pltpu.VMEM((part * node_blocks, 8, BLK), F32),
                pltpu.VMEM((3, BLK, BLK), F32),
                pltpu.VMEM((3, BLK, BLK), F32),
                pltpu.VMEM((3, BLK, BLK), jnp.int32),
                pltpu.VMEM((16, BLK), BF16),
                pltpu.VMEM((BLK, BLK), BF16),
                pltpu.VMEM((4, 8, count), F32),
                pltpu.SMEM((part * tile_count + 1,), jnp.int32),
                pltpu.SMEM((part * tile_count + 1,), jnp.int32),
            ],
            compiler_params=params,
            cost_estimate=pl.CostEstimate(
                flops=4_000_000_000, bytes_accessed=3_000_000, transcendentals=4_000_000
            ),
            name="bond",
        )(tiles, shift_now, broken_bits, surface_nodes, *listings)

    cut = grains * FIRST_SHARE // ALL_SHARES // GRAIN_UNROLL * GRAIN_UNROLL
    outgoing, shift_now = lax.optimization_barrier((outgoing, shift))
    received = lax.all_to_all(outgoing, ("grain", "cell"), split_axis=0, concat_axis=0, tiled=True)
    bond_a, place_a, pairs, order = bonds(0, cut, shift_now, pairs, send_order)
    received, bond_a, place_a = lax.optimization_barrier((received, bond_a, place_a))

    slot_force = pl.pallas_call(
        contact_kernel,
        out_shape=jax.ShapeDtypeStruct((owners, 3, share, BLK), F32),
        in_specs=[smem, smem, vmem],
        out_specs=vmem,
        scratch_shapes=[
            pltpu.VMEM((slots, 48, BLK), BF16),
            pltpu.VMEM((slots, 48, BLK), BF16),
            pltpu.VMEM((slots, 16, 2 * BLK), BF16),
            pltpu.VMEM((slots, 8, BLK), F32),
        ],
        compiler_params=params,
        name="contact",
    )(pairs, pair_count, received)

    slot_force, shift_now = lax.optimization_barrier((slot_force, shift_now))
    returned = lax.all_to_all(slot_force, ("grain", "cell"), split_axis=0, concat_axis=0, tiled=True)
    bond_b, place_b = bonds(cut, grains - cut, shift_now)

    force, new_speed = pl.pallas_call(
        functools.partial(finish_kernel, cut),
        out_shape=(jax.ShapeDtypeStruct((3, grains, count), F32),) * 2,
        in_specs=[smem, vmem, vmem, vmem, vmem, vmem, vmem],
        out_specs=(vmem, vmem),
        scratch_shapes=[pltpu.VMEM((3 * slots, BLK), F32)],
        compiler_params=params,
        name="finish",
    )(order, returned, place_a, bond_a, place_b, bond_b, speed)
    return force.transpose(1, 0, 2), new_speed.transpose(1, 0, 2)


def solution(mesh):
    own = ("grain", "cell")
    return jax.shard_map(
        on_device,
        mesh=mesh,
        in_specs=(
            P(own, None, None),
            P(own, None, None),
            P(None, own),
            P(own, None, None),
            P(own, None, None),
            P(own, None),
            P(own, None),
            P(own, None, None),
            P(own),
        ),
        out_specs=(P(own, None, None), P(own, None, None)),
        check_vma=False,
    )
```

```python
import functools
import math

import jax
import jax.numpy as jnp
from jax import lax
from jax.experimental import pallas as pl
from jax.experimental.pallas import tpu as pltpu
from jax.sharding import PartitionSpec as P

BLK = 128
HORIZON = 3.0
BOND_STIFF = 5.0
CONTACT_STIFF = 0.02
CONTACT_DAMP = 0.05
CONTACT_RANGE = 9.0
TIME_STEP = 0.5
VMEM_BYTES = 32 * 1024 * 1024
PICK_BYTES = 60 * 1024 * 1024
FAR = 100.0
BOND_UNROLL = 8
FAR_UNROLL = 4
PAIR_UNROLL = 16
GRAIN_UNROLL = 4
ROW_UNROLL = 4
OWNER_UNROLL = 4
FIRST_SHARE = 5
ALL_SHARES = 8
F32 = jnp.float32
BF16 = jnp.bfloat16


def iota(shape, axis):
    return lax.broadcasted_iota(jnp.int32, shape, axis)


def halves_of(number, size):
    if size & (size - 1):
        return lax.div(number, size), lax.rem(number, size)
    return number >> (size.bit_length() - 1), number & (size - 1)


def split3(value):
    one = value.astype(BF16).astype(F32)
    rest = value - one
    two = rest.astype(BF16).astype(F32)
    return one, two, (rest - two).astype(BF16).astype(F32)


def left_rows(value):
    one, two, three = split3(value)
    return jnp.concatenate([one, one, two, one, three, two], axis=0).astype(BF16)


def right_rows(value):
    one, two, three = split3(value)
    return jnp.concatenate([one, two, one, three, one, two], axis=0).astype(BF16)


def dot(left, right, left_dim, right_dim):
    return lax.dot_general(
        left, right, (((left_dim,), (right_dim,)), ((), ())), preferred_element_type=F32
    )


def split2(value):
    high = value.astype(BF16)
    return high, (value - high.astype(F32)).astype(BF16)


def stack_rows(pieces, width, kind=F32):
    row = iota((8, width), 0)
    total = jnp.zeros((8, width), kind)
    for number, piece in pieces.items():
        total = jnp.where(row == number, jnp.broadcast_to(piece, (8, width)), total)
    return total


def lattice_row(node):
    return (
        (node % 8).astype(F32) - 3.5,
        (node // 8 % 8).astype(F32) - 3.5,
        (node // 64).astype(F32) - 5.5,
    )


def pick_kernel(order, shift_in, velocity_in, centers, nodes_in, out, held, shift, velocity, nodes, arrived):
    copies = [
        pltpu.make_async_copy(source, target, arrived.at[number])
        for number, (source, target) in enumerate(
            ((shift_in, shift), (velocity_in, velocity), (nodes_in, nodes))
        )
    ]
    for copy in copies:
        copy.start()
    _, grains, count = shift.shape
    surface = nodes.shape[1]
    blocks = surface // BLK
    owners = out.shape[0]
    share = out.shape[1] // 6
    scale = math.sqrt(2.0 * math.log2(math.e) / CONTACT_RANGE)
    same = iota((grains, grains), 0) == iota((grains, grains), 1)
    offsets = [
        jnp.sum(jnp.where(same, centers[c : c + 1, :], 0.0), axis=1, keepdims=True)
        for c in range(3)
    ]
    for copy in copies:
        copy.wait()
    for group in range(grains // 8):
        rows = slice(group * 8, group * 8 + 8)
        places = []
        speeds = []
        for tile in range(count // BLK):
            span = slice(tile * BLK, tile * BLK + BLK)
            rest = lattice_row(iota((8, BLK), 1) + tile * BLK)
            now = [rest[c] + shift[c, rows, span] + offsets[c][rows] for c in range(3)]
            places.append([scale * now[c] for c in range(3)])
            speeds.append(
                [
                    CONTACT_STIFF * now[c] - CONTACT_DAMP * velocity[c, rows, span]
                    for c in range(3)
                ]
            )
        index = [nodes[rows, k * BLK : k * BLK + BLK] for k in range(blocks)]
        low = [one & (BLK - 1) for one in index]
        high = [one >> 7 for one in index]
        found = [[jnp.zeros((8, BLK), F32)] * 6 for _ in range(blocks)]
        for tile in range(count // BLK):
            sources = places[tile] + speeds[tile]
            for k in range(blocks):
                here = high[k] == tile
                found[k] = [
                    jnp.where(here, jnp.take_along_axis(sources[c], low[k], axis=1), found[k][c])
                    for c in range(6)
                ]
        for k in range(blocks):
            for c in range(6):
                base = (c * blocks + k) * grains + group * 8
                held[base : base + 8, :] = found[k][c]

    def send(n, carry):
        moved = []
        for u in range(ROW_UNROLL):
            d = n * ROW_UNROLL + u
            for cc in range(share):
                j = order[0, d * share + cc]
                grain, k = halves_of(j, blocks)
                row = k * grains + grain
                for c in range(6):
                    moved.append((d, cc * 6 + c, held[pl.ds(row + c * blocks * grains, 1), :]))
        for d, at, line in moved:
            out[d, at : at + 1, :] = line
        return carry

    lax.fori_loop(0, owners // ROW_UNROLL, send, 0)


def bond_kernel(first, grains, tiles, shift, bits, nodes, *refs):
    handed = (len(refs) - 15) // 2
    for listing, listing_out in zip(refs[:handed], refs[handed + 2 :]):
        listing_out[...] = listing[...]
    force, place = refs[handed : handed + 2]
    lefts, rights, sums, spots, total, inverse, square, dead, spread, fold, fixed, near, far = refs[-13:]
    count = shift.shape[2]
    tile_count = bits.shape[1]
    surface = nodes.shape[1]
    blocks = count // BLK

    q = iota((BLK, BLK), 0)
    p = iota((BLK, BLK), 1)
    flat = (q % 8 - p % 8) ** 2 + (q // 8 % 8 - p // 8 % 8) ** 2
    for delta in range(-1, 2):
        squared = (flat + (2 * delta + q // 64 - p // 64) ** 2).astype(F32)
        kept = (squared > 0.25) & (squared <= HORIZON * HORIZON)
        square[delta + 1] = jnp.where(kept, squared, FAR)
        inverse[delta + 1] = 1.0 / jnp.sqrt(jnp.where(kept, squared, FAR))
        dead[delta + 1] = jnp.where(kept, 0, 255)
    fold[...] = jnp.where(q // 16 == p % 8, 1.0, 0.0).astype(BF16)
    spread[...] = jnp.where(iota((16, BLK), 1) % 16 == iota((16, BLK), 0), 1.0, 0.0).astype(BF16)

    wide = (8, count)
    row = iota(wide, 0)
    rest = lattice_row(iota(wide, 1))
    rest_rows = jnp.where(row == 0, rest[0], jnp.where(row == 1, rest[1], jnp.where(row == 2, rest[2], 0.0)))
    fixed[0] = rest_rows
    fixed[1] = pltpu.roll(rest_rows, 3, 0) + jnp.where(row == 7, 1.0, 0.0)
    fixed[2] = rest_rows - jnp.where(row == 6, 0.5, 0.0)
    fixed[3] = rest_rows + jnp.where(row == 3, 1.0, 0.0)
    ids = iota((BLK, BLK), 0).astype(F32).astype(BF16)

    def prepare_one(g):
        moved = stack_rows({c: shift[c, pl.ds(first + g, 1), :] for c in range(3)}, count)
        own = jnp.sum(moved * (moved + 2.0 * fixed[0]), axis=0, keepdims=True)
        left = jnp.where(row == 6, own, moved + fixed[1])
        right = jnp.where(row == 7, own, -2.0 * (moved + pltpu.roll(moved, 3, 0) + fixed[2]))
        spot = moved + fixed[3]
        left_all = left_rows(left)
        right_all = right_rows(right)
        one, two, three = split3(spot)
        sum_all = jnp.concatenate([one, two, three, jnp.zeros_like(one)], axis=0).astype(BF16)

        listed = nodes[pl.ds(first + g, 1), :]
        low = (listed & (BLK - 1)).astype(F32).astype(BF16)
        high = listed >> 7
        position = iota((1, surface), 1)
        hit = iota((8, surface), 0) == jnp.broadcast_to(high, (8, surface))
        within = jnp.where(hit, jnp.broadcast_to((position % BLK + 1).astype(F32), (8, surface)), 0.0)
        group = jnp.where(hit, jnp.broadcast_to((position // BLK).astype(F32), (8, surface)), 0.0)
        chosen = jnp.concatenate([within, group], axis=0).astype(BF16)
        match = jnp.concatenate(
            [
                jnp.where(
                    ids == jnp.broadcast_to(low[:, k * BLK : k * BLK + BLK], (BLK, BLK)),
                    jnp.ones((BLK, BLK), BF16),
                    jnp.zeros((BLK, BLK), BF16),
                )
                for k in range(surface // BLK)
            ],
            axis=1,
        )
        found = dot(chosen, match, 1, 1)
        code = (found[:8] + float(BLK) * found[8:]).astype(jnp.int32)
        return left_all, right_all, sum_all, spot, code

    def prepare(n, carry):
        ready = [(n * GRAIN_UNROLL + u, prepare_one(n * GRAIN_UNROLL + u)) for u in range(GRAIN_UNROLL)]
        for g, (left_all, right_all, sum_all, spot, code) in ready:
            for h in range(blocks):
                span = slice(h * BLK, h * BLK + BLK)
                at = g * blocks + h
                lefts[at] = left_all[:, span]
                rights[at] = right_all[:, span]
                sums[at, :, :BLK] = sum_all[:, span]
                sums[at, :, BLK:] = sum_all[:, span]
                spots[at] = spot[:, span]
                total[at] = jnp.zeros((8, BLK), F32)
                place[pl.ds(h * grains + g, 1), :] = code[h : h + 1, :]
        return carry

    lax.fori_loop(0, grains // GRAIN_UNROLL, prepare, 0)

    def enlist(g, carry):
        near_held, far_held = carry
        for t in range(tile_count):
            gap = tiles[2 * t + 1, first + g] - tiles[2 * t, first + g]
            near[near_held] = g * tile_count + t
            far[far_held] = g * tile_count + t
            near_held = near_held + jnp.where((gap <= 1) & (gap >= -1), 1, 0)
            far_held = far_held + jnp.where((gap == 2) | (gap == -2), 1, 0)
        return near_held, far_held

    near_count, far_count = lax.fori_loop(0, grains, enlist, (0, 0))
    own_group = (iota((8, BLK), 1) // 16) == iota((8, BLK), 0)
    flag_all = jnp.left_shift(1, iota((BLK, BLK), 0) % 8)

    def step(n, carry):
        entries = []
        for u in range(BOND_UNROLL):
            number = n * BOND_UNROLL + u
            good = number < near_count
            entry = near[jnp.where(good, number, 0)]
            g, t = halves_of(entry, tile_count)
            a = tiles[2 * t, first + g]
            b = tiles[2 * t + 1, first + g]
            entries.append((good, g, t, g * blocks + a, g * blocks + b, b - a + 1))
        sorted_words = []
        for _, g, t, *_ in entries:
            words = bits[first + g, pl.ds(t, 1), :].astype(F32)
            for w in range(16):
                spread_row = jnp.broadcast_to(words[:, w * BLK : w * BLK + BLK], (8, BLK))
                sorted_words.append(jnp.where(own_group, spread_row, 0.0))
        sorted_words = jnp.concatenate(sorted_words, axis=0).astype(BF16)
        turned = dot(spread[...], sorted_words, 1, 1).astype(jnp.int32)
        halves = []
        for u, (_, _, _, row_at, col_at, delta) in enumerate(entries):
            excess = dot(lefts[col_at], rights[row_at], 0, 0)
            bond = inverse[delta] - lax.rsqrt(square[delta] + excess)
            own_flags = turned[:, u * BLK : u * BLK + BLK]
            flags = jnp.concatenate(
                [jnp.broadcast_to(own_flags[w : w + 1], (8, BLK)) for w in range(16)], axis=0
            )
            bond = jnp.where(((flags | dead[delta]) & flag_all) == 0, bond, 0.0)
            halves.append(jnp.concatenate(split2(bond), axis=0))
        results = []
        for u in range(0, BOND_UNROLL, 2):
            left = jnp.concatenate([sums[entries[v][4]] for v in (u, u + 1)], axis=0)
            both = dot(left, jnp.concatenate(halves[u : u + 2], axis=1), 1, 0)
            for v in range(2):
                good, _, _, row_at, _, _ = entries[u + v]
                found = both[v * 32 : v * 32 + 32, v * BLK : v * BLK + BLK]
                found = found[:8] + found[8:16] + found[16:24]
                gain = BOND_STIFF * (found - spots[row_at] * found[3:4])
                results.append((row_at, jnp.where(good, gain, 0.0)))
        for row_at, gain in results:
            total[row_at] = total[row_at] + gain
        return carry

    lax.fori_loop(0, (near_count + BOND_UNROLL - 1) // BOND_UNROLL, step, 0)

    lane = iota((8, BLK), 1)
    rank = iota((8, BLK), 0)
    turn = (lane % 64) // 8 == rank
    half_lane = iota((1, BLK), 1)

    def far_step(n, carry):
        results = []
        for u in range(FAR_UNROLL):
            number = n * FAR_UNROLL + u
            good = number < far_count
            entry = far[jnp.where(good, number, 0)]
            g, t = halves_of(entry, tile_count)
            a = tiles[2 * t, first + g]
            b = tiles[2 * t + 1, first + g]
            row_at = g * blocks + a
            col_at = g * blocks + b
            upper = jnp.where(b > a, 1, 0)
            own_words = bits[first + g, pl.ds(t, 1), pl.ds(pl.multiple_of(upper * 1024, 1024), 1024)]
            words = stack_rows(
                {r: own_words[:, r * BLK : r * BLK + BLK] for r in range(8)}, BLK, jnp.int32
            )
            flags = jnp.right_shift(words, lane // 16) & 1
            flags = jnp.where(lane % 16 == rank + 8 * (1 - upper), flags, 0).astype(F32)
            flags = jnp.concatenate([flags, jnp.zeros_like(flags)], axis=0).astype(BF16)
            flags = dot(flags, fold[...], 1, 0)[:8]
            broken = jnp.sum(jnp.where(turn, flags, 0.0), axis=0, keepdims=True)
            gap = pltpu.roll(spots[col_at], 64, 1) - spots[row_at]
            squares = gap * gap
            now_square = squares[0:1] + squares[1:2] + squares[2:3]
            bond = 1.0 / HORIZON - lax.rsqrt(now_square)
            kept = (half_lane // 64 == upper) & (broken < 0.5) & good
            bond = jnp.where(kept, BOND_STIFF * bond, 0.0)
            results.append((row_at, gap * bond))
        for row_at, gain in results:
            total[row_at] = total[row_at] + gain
        return carry

    lax.fori_loop(0, (far_count + FAR_UNROLL - 1) // FAR_UNROLL, far_step, 0)

    def finish(g, carry):
        for h in range(blocks):
            for c in range(3):
                force[pl.ds((c * blocks + h) * grains + g, 1), :] = total[g * blocks + h, c : c + 1, :]
        return carry

    lax.fori_loop(0, grains, finish, 0)


def contact_kernel(pairs, count, received, out, lefts, rights, sums, total):
    owners = received.shape[0]
    share = received.shape[1] // 6
    row = iota((8, BLK), 0)
    third = jnp.where(row == 3, 1.0, 0.0)
    fourth = jnp.where(row == 4, 1.0, 0.0)

    def prepare(n, carry):
        slots = range(OWNER_UNROLL * share)
        base = n * OWNER_UNROLL * share
        blank = jnp.zeros((2, BLK), F32)
        lines = []
        for u in slots:
            line = received[n * OWNER_UNROLL + u // share, u % share * 6 : u % share * 6 + 6, :]
            lines.append(jnp.concatenate([line, blank], axis=0))
        spots = [jnp.where(row < 3, line, 0.0) for line in lines]
        owns = [-0.5 * jnp.sum(spot * spot, axis=0, keepdims=True) for spot in spots]
        left = [left_rows(jnp.where(row == 3, own, spot + fourth)) for spot, own in zip(spots, owns)]
        right = [right_rows(jnp.where(row == 4, own, spot + third)) for spot, own in zip(spots, owns)]
        both = []
        for line in lines:
            high, low = split2(jnp.where(row == 6, 1.0, jnp.where(row < 3, 0.0, line)))
            both.append(jnp.concatenate([high.astype(F32), low.astype(F32)], axis=0).astype(BF16))
        for u in slots:
            at = base + u
            lefts[at] = left[u]
            rights[at] = right[u]
            sums[at, :, :BLK] = both[u]
            sums[at, :, BLK:] = both[u]
            total[at] = jnp.zeros((8, BLK), F32)
        return carry

    lax.fori_loop(0, owners // OWNER_UNROLL, prepare, 0)
    live = count[0]

    def step(n, carry):
        ready = []
        for u in range(PAIR_UNROLL):
            number = n * PAIR_UNROLL + u
            good = number < live
            at = jnp.where(good, number, 0)
            i = pairs[0, at]
            j = pairs[1, at]
            high, low = split2(jnp.exp2(dot(lefts[j], rights[i], 0, 0)))
            ready.append((i, j, good, high, low))
        results = []
        for u in range(0, PAIR_UNROLL, 2):
            two = ready[u : u + 2]
            upright = jnp.concatenate(
                [jnp.concatenate([high, low], axis=0) for *_, high, low in two], axis=1
            )
            flat = jnp.concatenate(
                [jnp.concatenate([high, low], axis=1) for *_, high, low in two], axis=0
            )
            gain_i = dot(jnp.concatenate([sums[j] for _, j, *_ in two], axis=0), upright, 1, 0)
            gain_j = dot(jnp.concatenate([sums[i] for i, *_ in two], axis=0), flat, 1, 1)
            for v, (i, j, good, _, _) in enumerate(two):
                span = slice(v * BLK, v * BLK + BLK)
                for at, gain in ((i, gain_i), (j, gain_j)):
                    gain = gain[v * 16 : v * 16 + 8, span] + gain[v * 16 + 8 : v * 16 + 16, span]
                    results.append((at, jnp.where(good, gain, 0.0)))
        for at, gain in results:
            total[at] = total[at] + gain
        return carry

    lax.fori_loop(0, (live + PAIR_UNROLL - 1) // PAIR_UNROLL, step, 0)

    def finish(n, carry):
        results = []
        for u in range(ROW_UNROLL):
            s = n * ROW_UNROLL + u
            for cc in range(share):
                found = total[s * share + cc]
                speeds = received[s, cc * 6 + 3 : cc * 6 + 6, :]
                results.append((s, cc, speeds * found[6:7] - found[3:6]))
        for s, cc, force in results:
            for c in range(3):
                out[s, c, cc : cc + 1, :] = force[c : c + 1]
        return carry

    lax.fori_loop(0, owners // ROW_UNROLL, finish, 0)


def finish_kernel(cut, order, returned, place_a, bond_a, place_b, bond_b, velocity, force, speed, held):
    _, grains, count = velocity.shape
    owners = returned.shape[0]
    node_blocks = count // BLK
    share = returned.shape[2]
    blocks = held.shape[0] // (3 * grains)

    def accept(n, carry):
        moved = []
        for u in range(ROW_UNROLL):
            d = n * ROW_UNROLL + u
            for cc in range(share):
                j = order[0, d * share + cc]
                grain, k = halves_of(j, blocks)
                row = k * grains + grain
                for c in range(3):
                    moved.append((row + c * blocks * grains, returned[d, c, cc : cc + 1, :]))
        for at, line in moved:
            held[pl.ds(at, 1), :] = line
        return carry

    lax.fori_loop(0, owners // ROW_UNROLL, accept, 0)

    def rows_of(early, late, group, part):
        start, end = group * 8, group * 8 + 8
        pieces = []
        if start < cut:
            pieces.append(early[part * cut + start : part * cut + min(end, cut), :])
        if end > cut:
            base = part * (grains - cut) - cut
            pieces.append(late[base + max(start, cut) : base + end, :])
        return pieces[0] if len(pieces) == 1 else jnp.concatenate(pieces, axis=0)

    for group in range(grains // 8):
        rows = slice(group * 8, group * 8 + 8)
        codes = [rows_of(place_a, place_b, group, tile) for tile in range(node_blocks)]
        low = [(code - 1) & (BLK - 1) for code in codes]
        high = [jnp.where(code == 0, -1, (code - 1) >> 7) for code in codes]
        found = [[jnp.zeros((8, BLK), F32)] * 3 for _ in codes]
        for k in range(blocks):
            sources = [
                held[(c * blocks + k) * grains + group * 8 : (c * blocks + k) * grains + group * 8 + 8, :]
                for c in range(3)
            ]
            for tile in range(node_blocks):
                here = high[tile] == k
                found[tile] = [
                    jnp.where(here, jnp.take_along_axis(sources[c], low[tile], axis=1), found[tile][c])
                    for c in range(3)
                ]
        for tile in range(node_blocks):
            span = slice(tile * BLK, tile * BLK + BLK)
            for c in range(3):
                total = rows_of(bond_a, bond_b, group, c * node_blocks + tile) + found[tile][c]
                force[c, rows, span] = total
                speed[c, rows, span] = velocity[c, rows, span] + TIME_STEP * total


def on_device(displacement, velocity, centers, tile_list, broken_bits, surface_nodes, send_order, pair_list, pair_count):
    grains, _, count = displacement.shape
    owners = lax.axis_size("grain") * lax.axis_size("cell")
    slots = send_order.shape[1]
    share = slots // owners
    surface = surface_nodes.shape[1]
    blocks = surface // BLK
    node_blocks = count // BLK
    tile_count = tile_list.shape[1]
    shift = displacement.transpose(1, 0, 2)
    speed = velocity.transpose(1, 0, 2)
    tiles = tile_list.transpose(1, 2, 0).reshape(2 * tile_count, grains)
    pairs = pair_list[0].T
    vmem = pl.BlockSpec(memory_space=pltpu.VMEM)
    smem = pl.BlockSpec(memory_space=pltpu.SMEM)
    hbm = pl.BlockSpec(memory_space=pltpu.HBM)
    params = pltpu.CompilerParams(vmem_limit_bytes=VMEM_BYTES)

    outgoing = pl.pallas_call(
        pick_kernel,
        out_shape=jax.ShapeDtypeStruct((owners, 6 * share, BLK), F32),
        in_specs=[smem, hbm, hbm, vmem, hbm],
        out_specs=vmem,
        scratch_shapes=[
            pltpu.VMEM((6 * slots, BLK), F32),
            pltpu.VMEM((3, grains, count), F32),
            pltpu.VMEM((3, grains, count), F32),
            pltpu.VMEM((grains, surface), jnp.int32),
            pltpu.SemaphoreType.DMA((3,)),
        ],
        compiler_params=pltpu.CompilerParams(vmem_limit_bytes=PICK_BYTES),
        name="pick",
    )(send_order, shift, speed, centers, surface_nodes)

    def bonds(first, part, shift_now, *listings):
        return pl.pallas_call(
            functools.partial(bond_kernel, first, part),
            out_shape=(
                jax.ShapeDtypeStruct((3 * node_blocks * part, BLK), F32),
                jax.ShapeDtypeStruct((node_blocks * part, BLK), jnp.int32),
                *[jax.ShapeDtypeStruct(listing.shape, jnp.int32) for listing in listings],
            ),
            in_specs=[smem, vmem, vmem, vmem] + [vmem] * len(listings),
            out_specs=(vmem,) * (2 + len(listings)),
            scratch_shapes=[
                pltpu.VMEM((part * node_blocks, 48, BLK), BF16),
                pltpu.VMEM((part * node_blocks, 48, BLK), BF16),
                pltpu.VMEM((part * node_blocks, 32, 2 * BLK), BF16),
                pltpu.VMEM((part * node_blocks, 8, BLK), F32),
                pltpu.VMEM((part * node_blocks, 8, BLK), F32),
                pltpu.VMEM((3, BLK, BLK), F32),
                pltpu.VMEM((3, BLK, BLK), F32),
                pltpu.VMEM((3, BLK, BLK), jnp.int32),
                pltpu.VMEM((16, BLK), BF16),
                pltpu.VMEM((BLK, BLK), BF16),
                pltpu.VMEM((4, 8, count), F32),
                pltpu.SMEM((part * tile_count + 1,), jnp.int32),
                pltpu.SMEM((part * tile_count + 1,), jnp.int32),
            ],
            compiler_params=params,
            cost_estimate=pl.CostEstimate(
                flops=4_000_000_000, bytes_accessed=3_000_000, transcendentals=4_000_000
            ),
            name="bond",
        )(tiles, shift_now, broken_bits, surface_nodes, *listings)

    cut = grains * FIRST_SHARE // ALL_SHARES // GRAIN_UNROLL * GRAIN_UNROLL
    outgoing, shift_now = lax.optimization_barrier((outgoing, shift))
    received = lax.all_to_all(outgoing, ("grain", "cell"), split_axis=0, concat_axis=0, tiled=True)
    bond_a, place_a, pairs, order = bonds(0, cut, shift_now, pairs, send_order)
    received, bond_a, place_a = lax.optimization_barrier((received, bond_a, place_a))

    slot_force = pl.pallas_call(
        contact_kernel,
        out_shape=jax.ShapeDtypeStruct((owners, 3, share, BLK), F32),
        in_specs=[smem, smem, vmem],
        out_specs=vmem,
        scratch_shapes=[
            pltpu.VMEM((slots, 48, BLK), BF16),
            pltpu.VMEM((slots, 48, BLK), BF16),
            pltpu.VMEM((slots, 16, 2 * BLK), BF16),
            pltpu.VMEM((slots, 8, BLK), F32),
        ],
        compiler_params=params,
        name="contact",
    )(pairs, pair_count, received)

    slot_force, shift_now = lax.optimization_barrier((slot_force, shift_now))
    returned = lax.all_to_all(slot_force, ("grain", "cell"), split_axis=0, concat_axis=0, tiled=True)
    bond_b, place_b = bonds(cut, grains - cut, shift_now)

    force, new_speed = pl.pallas_call(
        functools.partial(finish_kernel, cut),
        out_shape=(jax.ShapeDtypeStruct((3, grains, count), F32),) * 2,
        in_specs=[smem, vmem, vmem, vmem, vmem, vmem, vmem],
        out_specs=(vmem, vmem),
        scratch_shapes=[pltpu.VMEM((3 * slots, BLK), F32)],
        compiler_params=params,
        name="finish",
    )(order, returned, place_a, bond_a, place_b, bond_b, speed)
    return force.transpose(1, 0, 2), new_speed.transpose(1, 0, 2)


def solution(mesh):
    own = ("grain", "cell")
    return jax.shard_map(
        on_device,
        mesh=mesh,
        in_specs=(
            P(own, None, None),
            P(own, None, None),
            P(None, own),
            P(own, None, None),
            P(own, None, None),
            P(own, None),
            P(own, None),
            P(own, None, None),
            P(own),
        ),
        out_specs=(P(own, None, None), P(own, None, None)),
        check_vma=False,
    )
```
